512 devices in a mesh: row: 32 (over x, y, core), col: 16 (over z).
Axes of the slice: x: 4, y: 4, z: 16, core: 2. Of those that a mesh axis runs over, the one named last changes fastest.
Arguments:
- descriptors: bfloat16 [32, 98304], P(None, ('row', 'col')), may hold values from -6 to 6
- densities: float32 [98304], P(('row', 'col')), may hold values from 0.25 to 4
- vectors: float32 [32, 98304], P(None, ('row', 'col')), may hold values from -6 to 6
Outputs:
- next_block: float32 [32, 98304], P(None, ('row', 'col'))
The draws below stay inside these ranges and needn't reach their ends.
All inputs are finite; a program needn't handle non-finite values.
Results may differ from the reference program's by a relative error of at most 0.0036.
Values may be sent and summed in bfloat16 or wider, within the bound.
A program may use at most 64 MiB of HBM per device.

```python
import math
import jax
import jax.numpy as jnp
from jax import lax

FEAT = 32
VECS = 32
SAMPLES = 98304


def levels(rng, shape, cuts, smallest, high):
    factor_of = 1.0
    for dim, shards_of in cuts:
        heights = jax.random.uniform(jax.random.fold_in(jax.random.fold_in(rng, 6), dim), (shards_of,), jnp.float32, smallest / len(cuts), high / len(cuts))
        factor_of = factor_of * jnp.repeat(jnp.exp(heights), shape[dim] // shards_of).reshape((-1,) + (1,) * (len(shape) - 1 - dim))
    return factor_of


def normal_values(own_key, dims, scale, limit, cuts=(), held_as=jnp.bfloat16):
    values = jax.random.normal(own_key, dims, jnp.float32) * scale
    if len(cuts) > 0:
        values = levels(own_key, dims, cuts, -0.22, 0.18) * values
    return jnp.clip(values, min=-limit, max=limit).astype(held_as)


def setup_inputs(seed: int = 0) -> dict:
    key_list = jax.random.split(jax.random.key(seed), 4)
    return {
        "descriptors": normal_values(key_list[0], (FEAT, SAMPLES), 1.0, 6.0, ((1, 512),)),
        "densities": jnp.clip(jnp.exp(math.log(4.0) - 2.7725887 * jax.random.uniform(key_list[1], (SAMPLES,), jnp.float32) ** levels(key_list[1], (SAMPLES,), ((0, 512),), -0.2, 0.2)), 0.25, 4.0),
        "vectors": normal_values(key_list[2], (VECS, SAMPLES), 1.0, 6.0, ((1, 512),), jnp.float32),
    }


kernel_width = 8.0

def reference(descriptors, densities, vectors):
    highest = lax.Precision.HIGHEST
    features = descriptors.astype(jnp.float32)
    sq_norms = lax.optimization_barrier(jnp.sum(features * features, axis=0))
    weighted = (vectors / densities[None, :]).astype(jnp.bfloat16).astype(jnp.float32)
    inverse = (1.0 / densities).astype(jnp.bfloat16).astype(jnp.float32)[None, :]
    block_rows = math.gcd(SAMPLES, 1024)
    block_count = SAMPLES // block_rows
    blocked = features.reshape(FEAT, block_count, block_rows).transpose(1, 0, 2)
    norm_blocks = sq_norms.reshape(block_count, block_rows)

    def row_block(block_item):
        block_feat, block_norm = block_item
        inner_prod = jnp.dot(block_feat.T.astype(jnp.float32), features.astype(jnp.float32), precision=highest, preferred_element_type=jnp.float32)
        kernel = jnp.exp(-(block_norm[:, None] + sq_norms[None, :] - 2.0 * inner_prod) / kernel_width)
        kernel = kernel.astype(jnp.bfloat16).astype(jnp.float32)
        numerator = jnp.dot(weighted.astype(jnp.float32), kernel.T.astype(jnp.float32), precision=highest, preferred_element_type=jnp.float32)
        degree = jnp.dot(inverse.astype(jnp.float32), kernel.T.astype(jnp.float32), precision=highest, preferred_element_type=jnp.float32)
        return numerator / degree
    diffused = lax.map(row_block, (blocked, norm_blocks))
    diffused = diffused.transpose(1, 0, 2).reshape(VECS, SAMPLES)
    coupling = jnp.dot(vectors, diffused.T, precision=highest)
    remainder = diffused - jnp.dot(coupling.T, vectors, precision=highest) / SAMPLES
    spread = jnp.dot(remainder, remainder.T, precision=highest)
    factor = jnp.linalg.cholesky(spread)
    solved = jax.scipy.linalg.solve_triangular(factor, remainder, lower=True)
    return math.sqrt(SAMPLES) * solved
```

```python
import functools
import math

import jax
import jax.numpy as jnp
from jax import lax
from jax.experimental import pallas as pl
from jax.experimental.pallas import tpu as pltpu
from jax.sharding import PartitionSpec as P

MESH = pl.DeviceIdType.MESH
HIGHEST = lax.Precision.HIGHEST
F32, BF16 = jnp.float32, jnp.bfloat16

BLOCK = 192
PLANE = 16
DEPTH = 16
EXPONENT = math.log2(math.e) / 4.0


def norm_rows(x):
    half = 0.5 * jnp.sum(x * x, axis=0, keepdims=True)
    rest = jnp.broadcast_to(half, (16, half.shape[1]))
    at = lax.broadcasted_iota(jnp.int32, rest.shape, 0)
    rows = jnp.zeros_like(rest)
    for k in range(3):
        piece = rest.astype(BF16).astype(F32)
        rest = rest - piece
        rows = jnp.where(at == k, -piece, rows)
    return rows


def unit_rows(width):
    at = lax.broadcasted_iota(jnp.int32, (16, width), 0)
    return jnp.where(at < 3, 1.0, 0.0)


def lower_inverse(spread):
    n = spread.shape[0]
    at_row = lax.broadcasted_iota(jnp.int32, (n, 2 * n), 0)
    at_col = lax.broadcasted_iota(jnp.int32, (n, 2 * n), 1)
    both = jnp.concatenate([spread, spread], axis=1)
    work = jnp.where(at_col < n, both, jnp.where(at_col - n == at_row, 1.0, 0.0))
    for k in range(n):
        pivot_row = work[k : k + 1, :]
        inverse = lax.rsqrt(work[k : k + 1, k : k + 1])
        pivot_row = pivot_row * inverse
        column = work[:, k : k + 1] * inverse
        work = jnp.where(
            at_row > k, work - column * pivot_row, jnp.where(at_row == k, pivot_row, work)
        )
    return work[:, n:]


def kernel(
    desc_ref, dens_ref, vec_ref, out_ref,
    ring, sib, feats, tgt, wts, acc, parts_out, parts_in, held, tiles, slices_in, sums_in, total_in,
    ring_s, ring_r, sib_s, sib_r, tgt_s, tgt_r, part_s, part_r, ga_s, ga_r, gb_s, gb_r, gc_s, gc_r,
):
    row, z = lax.axis_index("row"), lax.axis_index("col")
    p, c = row // 2, row % 2
    other = 1 - c
    up, down = (z + 1) % DEPTH, (z + DEPTH - 1) % DEPTH
    half = p // 8
    samples = float(BLOCK * PLANE * DEPTH * 2)

    barrier = pltpu.get_barrier_semaphore()

    def greet(device):
        pl.semaphore_signal(barrier, inc=1, device_id=device, device_id_type=MESH)

    def greet_near(k, _):
        greet((((p + k) % PLANE) * 2 + c, z))
        greet((row, (z + k) % DEPTH))
        return 0

    lax.fori_loop(1, 16, greet_near, 0)

    def greet_half(k, _):
        greet(((half * 8 + k) * 2 + other, z))
        return 0

    lax.fori_loop(0, 8, greet_half, 0)
    greet((p * 2 + other, down))

    x = desc_ref[...].astype(F32)
    pieces = norm_rows(x)
    units = unit_rows(BLOCK)
    pad = lambda v: jnp.concatenate([v, jnp.zeros((v.shape[0], 256 - BLOCK), v.dtype)], axis=1)
    source = pad(jnp.concatenate([x, pieces, units], axis=0))
    later = pltpu.roll(source, 160, 1)
    packed = jnp.concatenate([source[:, :128], later[:, :128]], axis=0).T[:96]
    inverse = 1.0 / dens_ref[...]
    at16 = lax.broadcasted_iota(jnp.int32, (16, BLOCK), 0)
    vec = vec_ref[...]
    cols = pad(
        jnp.concatenate(
            [vec / dens_ref[...], jnp.where(at16 == 0, jnp.broadcast_to(inverse, (16, BLOCK)), 0.0)],
            axis=0,
        )
    )
    for d in range(2):
        ring[d, 0, 0:96] = packed.astype(BF16)
        ring[d, 0, 96:144] = cols[:, :128].astype(BF16)
        tail = cols[:, 128:]
        ring[d, 0, 144:192] = (pltpu.roll(tail, 64, 1) if d else tail).astype(BF16)
    sib[0, 0] = ring[0, 0]
    target = pad(jnp.concatenate([x, pieces], axis=0))
    odd = (p % 2) == 1
    tail = target[:, 128:]
    feats[p, 0:48] = target[:, :128].astype(BF16)
    feats[p, 48:96] = jnp.where(odd, pltpu.roll(tail, 64, 1), tail).astype(BF16)

    pl.semaphore_wait(barrier, 39)

    def ring_copy(d, r):
        if d == 0:
            device = (row, down)
        else:
            device = (p * 2 + jnp.where(r == 7, other, c), up)
        return pltpu.make_async_remote_copy(
            src_ref=ring.at[d, r], dst_ref=ring.at[d, r + 1],
            send_sem=ring_s.at[d, r], recv_sem=ring_r.at[d, r + 1],
            device_id=device, device_id_type=MESH,
        )

    def sib_copy(d, r):
        return pltpu.make_async_remote_copy(
            src_ref=ring.at[d, r], dst_ref=sib.at[d, r],
            send_sem=sib_s.at[d, r], recv_sem=sib_r.at[d, r],
            device_id=(p * 2 + other, z), device_id_type=MESH,
        )

    def tgt_copy(k):
        q = (p + k) % PLANE
        return pltpu.make_async_remote_copy(
            src_ref=feats.at[p], dst_ref=feats.at[p],
            send_sem=tgt_s.at[k], recv_sem=tgt_r.at[k],
            device_id=(q * 2 + c, z), device_id_type=MESH,
        )

    ring_copy(0, 0).start()
    ring_copy(1, 0).start()
    sib_copy(1, 0).start()

    def send_tgt(k, _):
        tgt_copy(k).start()
        return 0

    lax.fori_loop(1, 16, send_tgt, 0)
    acc[...] = jnp.zeros_like(acc)

    def wait_tgt(k, _):
        q = (p + PLANE - k) % PLANE
        pltpu.make_async_remote_copy(
            src_ref=feats.at[q], dst_ref=feats.at[q],
            send_sem=tgt_s.at[k], recv_sem=tgt_r.at[k],
            device_id=(q * 2 + c, z), device_id_type=MESH,
        ).wait_recv()
        return 0

    lax.fori_loop(1, 16, wait_tgt, 0)

    unit_tile = unit_rows(128).astype(BF16)
    zeros = jnp.zeros((64, 128), BF16)

    def build_tgt(pair, _):
        first, second = 2 * pair, 2 * pair + 1
        tile3 = (
            feats[first, 0:48],
            feats[second, 0:48],
            feats[first, 48:96] + feats[second, 48:96],
        )
        for t in range(3):
            tiles[3 * pair + t] = jnp.concatenate(
                [tile3[t][:32], unit_tile, tile3[t][32:48], zeros], axis=0
            )
        return 0

    lax.fori_loop(0, 8, build_tgt, 0)
    for k in range(12):
        tgt[k] = jnp.concatenate([tiles[2 * k], tiles[2 * k + 1]], axis=1)

    def unpack(first, second, base):
        for s, block in ((0, first), (1, second)):
            packed = block[0:96]
            held[base + 128 * s : base + 128 * s + 96, :] = packed
            packed = pltpu.roll(packed.astype(F32), 64, 1).astype(BF16)
            held[base + 128 * s + 96 : base + 128 * s + 128, :] = packed[0:32]
            held[base + 256 + 64 * s : base + 320 + 64 * s, :] = packed[32:96]
        wts[:, base : base + 128] = first[96:144]
        wts[:, base + 128 : base + 256] = second[96:144]
        wts[:, base + 256 : base + 384] = first[144:192] + second[144:192]

    def step(b, _):
        for d in range(2):
            ring_copy(d, b).wait_recv()

        @pl.when(b < 7)
        def _():
            for d in range(2):
                ring_copy(d, b + 1).start()
            for d in range(2):
                sib_copy(d, b + 1).start()

        @pl.when(b > 0)
        def _():
            sib_copy(0, b).wait_recv()

        sib_copy(1, b).wait_recv()
        unpack(ring[0, b + 1], ring[1, b + 1], 0)
        unpack(sib[0, b], sib[1, b], 384)
        rows = held[...]
        weights = wts[...]

        kernels, inner = {}, {}
        for k in range(14):
            if k < 12:
                inner[k] = jnp.dot(rows, tgt[k], preferred_element_type=F32)
            if 0 <= k - 1 < 12:
                kernels[k - 1] = jnp.exp2(inner.pop(k - 1) * F32(EXPONENT)).astype(BF16)
            if 0 <= k - 2 < 12:
                acc[k - 2] += jnp.dot(weights, kernels.pop(k - 2), preferred_element_type=F32)
        return 0

    lax.fori_loop(0, 8, step, 0)

    for pair in range(8):
        tile3 = []
        for t in range(3):
            tile = 3 * pair + t
            tile3.append(acc[tile // 2, :, (tile % 2) * 128 : (tile % 2) * 128 + 128].astype(BF16))
        for s in range(2):
            parts_out[2 * pair + s, 0:48] = tile3[s]
            parts_out[2 * pair + s, 48:96] = tile3[2]

    def part_copy(k):
        q = (p + k) % PLANE
        return pltpu.make_async_remote_copy(
            src_ref=parts_out.at[q], dst_ref=parts_in.at[k],
            send_sem=part_s.at[k], recv_sem=part_r.at[k],
            device_id=(q * 2 + c, z), device_id_type=MESH,
        )

    def send_part(k, _):
        part_copy(k).start()
        return 0

    lax.fori_loop(1, 16, send_part, 0)
    sums = parts_out[p].astype(F32)
    for k in range(1, 16):
        part_copy(k).wait_recv()
        sums = sums + parts_in[k].astype(F32)
    tail = sums[48:96]
    tail = jnp.where(odd, pltpu.roll(tail, 64, 1), tail)
    sums = jnp.concatenate([sums[0:48], tail], axis=1)[:, :BLOCK]
    diffused = sums[0:32] / sums[32:33]

    stacked = jnp.concatenate([vec, diffused], axis=0)
    gram = lax.dot_general(
        stacked, stacked, (((1,), (1,)), ((), ())), precision=HIGHEST, preferred_element_type=F32
    )
    gram = jnp.concatenate([gram, jnp.zeros((64, 64), F32)], axis=1)
    slices = slices_in.at[1]
    for j in range(8):
        slices[j] = gram[8 * j : 8 * j + 8]

    def ga_copy(k):
        q = (p + k) % PLANE
        return pltpu.make_async_remote_copy(
            src_ref=slices_in.at[1, q % 8], dst_ref=slices_in.at[0, k],
            send_sem=ga_s.at[k], recv_sem=ga_r.at[k],
            device_id=(q * 2 + c, z), device_id_type=MESH,
        )

    def send_ga(k, _):
        ga_copy(k).start()
        return 0

    lax.fori_loop(1, 16, send_ga, 0)
    part = slices_in[1, p % 8]
    for k in range(1, 16):
        ga_copy(k).wait_recv()
        part = part + slices_in[0, k]
    sums_in[0] = part

    def gb_copy(k):
        return pltpu.make_async_remote_copy(
            src_ref=sums_in.at[0], dst_ref=sums_in.at[k],
            send_sem=gb_s.at[k], recv_sem=gb_r.at[k],
            device_id=(row, (z + k) % DEPTH), device_id_type=MESH,
        )

    def send_gb(k, _):
        gb_copy(k).start()
        return 0

    lax.fori_loop(1, 16, send_gb, 0)
    for k in range(1, 16):
        gb_copy(k).wait_recv()
        part = part + sums_in[k]

    mine = p % 8
    total_in[c, mine] = part

    def gc_copy(s, k):
        q = half * 8 + (mine + k) % 8
        core = c if s == 0 else other
        return pltpu.make_async_remote_copy(
            src_ref=total_in.at[c, mine], dst_ref=total_in.at[c, mine],
            send_sem=gc_s.at[s, k], recv_sem=gc_r.at[s, k],
            device_id=(q * 2 + core, z), device_id_type=MESH,
        )

    def gc_recv(s, k):
        slot = (mine + 8 - k) % 8
        core = c if s == 0 else other
        return pltpu.make_async_remote_copy(
            src_ref=total_in.at[core, slot], dst_ref=total_in.at[core, slot],
            send_sem=gc_s.at[s, k], recv_sem=gc_r.at[s, k],
            device_id=(row, z), device_id_type=MESH,
        )

    def send_gc(k, _):
        gc_copy(1, k).start()

        @pl.when(k > 0)
        def _():
            gc_copy(0, k).start()

        return 0

    lax.fori_loop(0, 8, send_gc, 0)

    def wait_gc(k, _):
        gc_recv(1, k).wait_recv()

        @pl.when(k > 0)
        def _():
            gc_recv(0, k).wait_recv()

        return 0

    lax.fori_loop(0, 8, wait_gc, 0)
    total = (total_in[0] + total_in[1]).reshape(64, 128)
    basis, coupling, square = total[:32, :32], total[:32, 32:64], total[32:, 32:64]
    dot_t = lambda a, b: lax.dot_general(
        a, b, (((0,), (0,)), ((), ())), precision=HIGHEST, preferred_element_type=F32
    )
    mixed = jnp.dot(basis, coupling, precision=HIGHEST, preferred_element_type=F32)
    spread = square + dot_t(
        coupling, mixed * (1.0 / (samples * samples)) - coupling * (2.0 / samples)
    )
    remainder = diffused - dot_t(coupling, vec) * (1.0 / samples)
    factor = lower_inverse(spread)
    out_ref[...] = math.sqrt(samples) * jnp.dot(
        factor, remainder, precision=HIGHEST, preferred_element_type=F32
    )

    for d in range(2):
        def wait_ring(r, _):
            ring_copy(d, r).wait_send()
            return 0

        lax.fori_loop(0, 8, wait_ring, 0)

        def wait_sib(r, _):
            sib_copy(d, r).wait_send()
            return 0

        lax.fori_loop(1 - d, 8, wait_sib, 0)

    def wait_sent(k, _):
        tgt_copy(k).wait_send()
        part_copy(k).wait_send()
        ga_copy(k).wait_send()
        gb_copy(k).wait_send()
        return 0

    lax.fori_loop(1, 16, wait_sent, 0)

    def wait_gc_sent(k, _):
        gc_copy(1, k).wait_send()

        @pl.when(k > 0)
        def _():
            gc_copy(0, k).wait_send()

        return 0

    lax.fori_loop(0, 8, wait_gc_sent, 0)


def per_device(descriptors, densities, vectors):
    dma = pltpu.SemaphoreType.DMA
    return pl.pallas_call(
        kernel,
        out_shape=jax.ShapeDtypeStruct((32, BLOCK), F32),
        in_specs=[pl.BlockSpec(memory_space=pltpu.VMEM)] * 3,
        out_specs=pl.BlockSpec(memory_space=pltpu.VMEM),
        scratch_shapes=[
            pltpu.VMEM((2, 9, 192, 128), BF16),
            pltpu.VMEM((2, 8, 192, 128), BF16),
            pltpu.VMEM((16, 96, 128), BF16),
            pltpu.VMEM((12, 128, 256), BF16),
            pltpu.VMEM((48, 768), BF16),
            pltpu.VMEM((12, 48, 256), F32),
            pltpu.VMEM((16, 96, 128), BF16),
            pltpu.VMEM((16, 96, 128), BF16),
            pltpu.VMEM((768, 128), BF16),
            pltpu.VMEM((24, 128, 128), BF16),
            pltpu.VMEM((2, 16, 8, 128), F32),
            pltpu.VMEM((16, 8, 128), F32),
            pltpu.VMEM((2, 8, 8, 128), F32),
            dma((2, 9)), dma((2, 9)), dma((2, 8)), dma((2, 8)),
            dma((16,)), dma((16,)), dma((16,)), dma((16,)),
            dma((16,)), dma((16,)), dma((16,)), dma((16,)),
            dma((2, 8)), dma((2, 8)),
        ],
        compiler_params=pltpu.CompilerParams(
            collective_id=0, has_side_effects=True, vmem_limit_bytes=48 << 20
        ),
    )(descriptors, densities.reshape(1, BLOCK), vectors)


def solution(mesh):
    placed = P(None, ("row", "col"))
    return jax.shard_map(
        per_device,
        mesh=mesh,
        in_specs=(placed, P(("row", "col")), placed),
        out_specs=placed,
        check_vma=False,
    )
```

```python
import functools
import math

import jax
import jax.numpy as jnp
from jax import lax
from jax.experimental import pallas as pl
from jax.experimental.pallas import tpu as pltpu
from jax.sharding import PartitionSpec as P

MESH = pl.DeviceIdType.MESH
HIGHEST = lax.Precision.HIGHEST
F32, BF16 = jnp.float32, jnp.bfloat16

BLOCK = 192
PLANE = 16
DEPTH = 16
EXPONENT = math.log2(math.e) / 4.0


def norm_rows(x):
    half = 0.5 * jnp.sum(x * x, axis=0, keepdims=True)
    rest = jnp.broadcast_to(half, (16, half.shape[1]))
    at = lax.broadcasted_iota(jnp.int32, rest.shape, 0)
    rows = jnp.zeros_like(rest)
    for k in range(3):
        piece = rest.astype(BF16).astype(F32)
        rest = rest - piece
        rows = jnp.where(at == k, -piece, rows)
    return rows


def unit_rows(width):
    at = lax.broadcasted_iota(jnp.int32, (16, width), 0)
    return jnp.where(at < 3, 1.0, 0.0)


def lower_inverse(spread):
    n = spread.shape[0]
    at_row = lax.broadcasted_iota(jnp.int32, (n, 2 * n), 0)
    at_col = lax.broadcasted_iota(jnp.int32, (n, 2 * n), 1)
    both = jnp.concatenate([spread, spread], axis=1)
    work = jnp.where(at_col < n, both, jnp.where(at_col - n == at_row, 1.0, 0.0))
    for k in range(n):
        pivot_row = work[k : k + 1, :]
        inverse = lax.rsqrt(work[k : k + 1, k : k + 1])
        pivot_row = pivot_row * inverse
        column = work[:, k : k + 1] * inverse
        work = jnp.where(
            at_row > k, work - column * pivot_row, jnp.where(at_row == k, pivot_row, work)
        )
    return work[:, n:]


NEAR = sorted(
    ((dx, dy) for dx in range(4) for dy in range(4)),
    key=lambda o: min(o[0], 4 - o[0]) + min(o[1], 4 - o[1]),
)
PAIRS = ((2, -1), (1, 0), (4, -3), (3, -2), (8, -7), (7, -6), (6, -5), (5, -4))
REACH = 4


def kernel(
    desc_ref, dens_ref, vec_ref, out_ref,
    src, feats, tgt, wts, acc, parts_out, parts_in, slices_in, sums_in, total_in,
    src_s, src_r, sib_s, sib_r, tgt_s, tgt_r, part_s, part_r, ga_s, ga_r, gb_s, gb_r, gc_s, gc_r,
):
    row, z = lax.axis_index("row"), lax.axis_index("col")
    p, c = row // 2, row % 2
    px, py = p // 4, p % 4
    other = 1 - c
    half = p // 8
    samples = float(BLOCK * PLANE * DEPTH * 2)

    def chip(dx, dy):
        return ((px + dx) % 4) * 4 + (py + dy) % 4

    def along(d):
        return (z + d + DEPTH) % DEPTH

    barrier = pltpu.get_barrier_semaphore()

    def greet(device):
        pl.semaphore_signal(barrier, inc=1, device_id=device, device_id_type=MESH)

    for d in range(1, REACH + 1):
        greet((row, along(d)))
        greet((row, along(-d)))
    for dx, dy in NEAR[1:]:
        greet((chip(dx, dy) * 2 + c, z))
    greet((p * 2 + other, z))

    lane16 = lax.broadcasted_iota(jnp.int32, (16, 128), 1)
    at16 = lax.broadcasted_iota(jnp.int32, (16, 128), 0)
    turn = lambda v: pltpu.roll(v, 64, 1)
    pad = lambda v: jnp.concatenate([v, jnp.zeros((v.shape[0], 256 - BLOCK), v.dtype)], axis=1)

    def fold(v):
        return jnp.where(lane16 < 64, v[:16], turn(v[16:]))

    def merge(first, second):
        return jnp.concatenate(
            [jnp.where(lane16 < 64, first, turn(second)), jnp.where(lane16 < 64, turn(first), second)],
            axis=0,
        )

    x = pad(desc_ref[...].astype(F32))
    feats[7, 0:32] = x[:, :128].astype(BF16)
    feats[7, 32:48] = fold(x[:, 128:]).astype(BF16)
    source = jnp.concatenate([x, norm_rows(x), unit_rows(256)], axis=0)
    later = pltpu.roll(source, 160, 1)
    packed = jnp.concatenate([source[:, :128], later[:, :128]], axis=0).T[:96]
    src[0, 0, 0:96] = packed.astype(BF16)
    vec = vec_ref[...]
    inverse = pad(1.0 / dens_ref[...])
    weighted = pad(vec / dens_ref[...])
    src[0, 0, 96:128] = weighted[:, :128].astype(BF16)
    src[0, 0, 128:144] = fold(weighted[:, 128:]).astype(BF16)
    tail = jnp.broadcast_to(inverse[:, 128:], (16, 128))
    src[0, 0, 144:160] = jnp.where(
        at16 == 0,
        jnp.broadcast_to(inverse[:, :128], (16, 128)),
        jnp.where(at16 == 1, jnp.where(lane16 < 64, tail, turn(tail)), 0.0),
    ).astype(BF16)

    pl.semaphore_wait(barrier, 2 * REACH + 16)

    def remote(source_ref, target_ref, send_sem, recv_sem, device):
        return pltpu.make_async_remote_copy(
            src_ref=source_ref, dst_ref=target_ref, send_sem=send_sem, recv_sem=recv_sem,
            device_id=device, device_id_type=MESH,
        )

    def src_copy(j):
        return remote(
            src.at[0, 0], src.at[0, j], src_s.at[j], src_r.at[j], (chip(*NEAR[j]) * 2 + c, z)
        )

    def sib_copy(j):
        return remote(
            src.at[0, j], src.at[1, j], sib_s.at[j], sib_r.at[j], (p * 2 + other, z)
        )

    def tgt_copy(e):
        if abs(e) <= REACH:
            return remote(
                feats.at[7], feats.at[7 + e], tgt_s.at[7 + e], tgt_r.at[7 + e], (row, along(-e))
            )
        step = REACH if e > 0 else -REACH
        return remote(
            feats.at[7 + e - step], feats.at[7 + e], tgt_s.at[7 + e], tgt_r.at[7 + e],
            (row, along(-step)),
        )

    near = [e for d in range(1, REACH + 1) for e in (d, -d)]
    far = [e for d in range(1, REACH + 1) for e in (d + REACH, -d - REACH) if e > -8]
    for e in near:
        tgt_copy(e).start()
    sib_copy(0).start()
    for j in range(1, 16):
        src_copy(j).start()
    acc[...] = jnp.zeros_like(acc)
    for e in near:
        tgt_copy(e).wait_recv()
        ahead = e + (REACH if e > 0 else -REACH)
        if ahead in far:
            tgt_copy(ahead).start()

    unit_tile = unit_rows(128)
    zeros = jnp.zeros((64, 128), F32)

    def build(pair):
        first, second = (feats[7 + e].astype(F32) for e in PAIRS[pair])
        for t, tile in enumerate((first[:32], second[:32], merge(first[32:], second[32:]))):
            rows = jnp.concatenate([tile, unit_tile, norm_rows(tile)], axis=0)
            k = 3 * pair + t
            at = slice(128 * (k % 2), 128 * (k % 2) + 128)
            tgt[0, k // 2, :, at] = jnp.concatenate([rows, zeros], axis=0).astype(BF16)
            tgt[1, k // 2, :, at] = jnp.concatenate([zeros, rows], axis=0).astype(BF16)

    for pair in range(4):
        build(pair)

    def columns(j):
        first, second = src[0, j], src[1, j]
        wts[j, :, 0:128] = jnp.concatenate([first[96:128], first[144:160]], axis=0)
        wts[j, :, 128:256] = jnp.concatenate([second[96:128], second[144:160]], axis=0)
        tails = merge(first[128:144].astype(F32), second[128:144].astype(F32))
        ends = jnp.where(
            lane16 < 64, first[144:160].astype(F32), second[144:160].astype(F32)
        )
        ends = jnp.where(at16 == 0, jnp.broadcast_to(ends[1:2], (16, 128)), 0.0)
        wts[j, :, 256:384] = jnp.concatenate([tails, ends], axis=0).astype(BF16)

    def work(first_chunk, m):
        units = [(k, n) for k in range(6) for n in range(2)]
        inner, kernels = {}, {}
        for i in range(len(units) + 2):
            if i < len(units):
                k, n = units[i]
                rows = jnp.concatenate(
                    [src[s, 4 * m + 2 * n + j, 0:96] for j in range(2) for s in range(2)], axis=0
                )
                inner[i] = [
                    jnp.dot(rows, tgt[v, first_chunk + k], preferred_element_type=F32)
                    for v in range(2)
                ]
            if 0 <= i - 1 < len(units):
                low, high = (
                    jnp.exp2(u * F32(EXPONENT)).astype(BF16) for u in inner.pop(i - 1)
                )
                order = []
                for j in range(2):
                    a, b = 192 * j, 192 * j + 96
                    order += [
                        low[a : a + 96], high[a : a + 32], low[b : b + 96], high[b : b + 32],
                        high[a + 32 : a + 96], high[b + 32 : b + 96],
                    ]
                kernels[i - 1] = jnp.concatenate(order, axis=0)
            if 0 <= i - 2 < len(units):
                k, n = units[i - 2]
                weights = jnp.concatenate(
                    [wts[4 * m + 2 * n + j] for j in range(2)], axis=1
                )
                acc[first_chunk + k] += jnp.dot(
                    weights, kernels.pop(i - 2), preferred_element_type=F32
                )

    def part_copy(e):
        return remote(
            parts_out.at[7 + e], parts_in.at[7 + e], part_s.at[7 + e], part_r.at[7 + e],
            (row, along(e)),
        )

    def send_parts(pair):
        tiles = [
            acc[k // 2, :, 128 * (k % 2) : 128 * (k % 2) + 128]
            for k in range(3 * pair, 3 * pair + 3)
        ]
        both = tiles[2]
        for s, e in enumerate(PAIRS[pair]):
            tail = turn(both) if s else both
            parts_out[7 + e, 0:32] = tiles[s][:32].astype(BF16)
            parts_out[7 + e, 32:48] = fold(tail[:32]).astype(BF16)
            parts_out[7 + e, 48:64] = jnp.where(
                at16 == 0,
                jnp.broadcast_to(tiles[s][32:33], (16, 128)),
                jnp.broadcast_to(tail[32:33], (16, 128)),
            ).astype(BF16)
            if e != 0:
                part_copy(e).start()

    def arrive(m):
        for j in range(4 * m, 4 * m + 4):
            if j > 0:
                src_copy(j).wait_recv()
                sib_copy(j).start()

    arrive(0)
    for m in range(4):
        if m < 3:
            arrive(m + 1)
        for j in range(4 * m, 4 * m + 4):
            sib_copy(j).wait_recv()
            columns(j)
        work(0, m)
    for pair in range(4):
        send_parts(pair)
    for e in far:
        tgt_copy(e).wait_recv()
    for pair in range(4, 8):
        build(pair)

    def second(m, _):
        work(6, m)
        return 0

    lax.fori_loop(0, 4, second, 0)
    for pair in range(4, 8):
        send_parts(pair)
    sums = parts_out[7].astype(F32)
    ups = [e for pair in PAIRS for e in pair if e != 0]
    for e in ups:
        part_copy(e).wait_recv()
        sums = sums + parts_in[7 + e].astype(F32)
    tail = sums[32:48]
    tail = jnp.concatenate([tail, turn(tail)], axis=0)
    top = jnp.concatenate([sums[:32], tail], axis=1)[:, :BLOCK]
    degree = jnp.concatenate([sums[48:49], sums[49:50]], axis=1)[:, :BLOCK]
    diffused = top / degree

    stacked = jnp.concatenate([vec, diffused], axis=0)
    gram = lax.dot_general(
        stacked, stacked, (((1,), (1,)), ((), ())), precision=HIGHEST, preferred_element_type=F32
    )
    gram = jnp.concatenate([gram, jnp.zeros((64, 64), F32)], axis=1)
    slices = slices_in.at[1]
    for j in range(8):
        slices[j] = gram[8 * j : 8 * j + 8]

    def ga_copy(k):
        q = (p + k) % PLANE
        return pltpu.make_async_remote_copy(
            src_ref=slices_in.at[1, q % 8], dst_ref=slices_in.at[0, k],
            send_sem=ga_s.at[k], recv_sem=ga_r.at[k],
            device_id=(q * 2 + c, z), device_id_type=MESH,
        )

    def send_ga(k, _):
        ga_copy(k).start()
        return 0

    lax.fori_loop(1, 16, send_ga, 0)
    part = slices_in[1, p % 8]
    for k in range(1, 16):
        ga_copy(k).wait_recv()
        part = part + slices_in[0, k]
    sums_in[0] = part

    def gb_copy(k):
        return pltpu.make_async_remote_copy(
            src_ref=sums_in.at[0], dst_ref=sums_in.at[k],
            send_sem=gb_s.at[k], recv_sem=gb_r.at[k],
            device_id=(row, (z + k) % DEPTH), device_id_type=MESH,
        )

    def send_gb(k, _):
        gb_copy(k).start()
        return 0

    lax.fori_loop(1, 16, send_gb, 0)
    for k in range(1, 16):
        gb_copy(k).wait_recv()
        part = part + sums_in[k]

    mine = p % 8
    total_in[c, mine] = part

    def gc_copy(s, k):
        q = half * 8 + (mine + k) % 8
        core = c if s == 0 else other
        return pltpu.make_async_remote_copy(
            src_ref=total_in.at[c, mine], dst_ref=total_in.at[c, mine],
            send_sem=gc_s.at[s, k], recv_sem=gc_r.at[s, k],
            device_id=(q * 2 + core, z), device_id_type=MESH,
        )

    def gc_recv(s, k):
        slot = (mine + 8 - k) % 8
        core = c if s == 0 else other
        return pltpu.make_async_remote_copy(
            src_ref=total_in.at[core, slot], dst_ref=total_in.at[core, slot],
            send_sem=gc_s.at[s, k], recv_sem=gc_r.at[s, k],
            device_id=(row, z), device_id_type=MESH,
        )

    def send_gc(k, _):
        gc_copy(1, k).start()

        @pl.when(k > 0)
        def _():
            gc_copy(0, k).start()

        return 0

    lax.fori_loop(0, 8, send_gc, 0)

    def wait_gc(k, _):
        gc_recv(1, k).wait_recv()

        @pl.when(k > 0)
        def _():
            gc_recv(0, k).wait_recv()

        return 0

    lax.fori_loop(0, 8, wait_gc, 0)
    total = (total_in[0] + total_in[1]).reshape(64, 128)
    basis, coupling, square = total[:32, :32], total[:32, 32:64], total[32:, 32:64]
    dot_t = lambda a, b: lax.dot_general(
        a, b, (((0,), (0,)), ((), ())), precision=HIGHEST, preferred_element_type=F32
    )
    mixed = jnp.dot(basis, coupling, precision=HIGHEST, preferred_element_type=F32)
    spread = square + dot_t(
        coupling, mixed * (1.0 / (samples * samples)) - coupling * (2.0 / samples)
    )
    remainder = diffused - dot_t(coupling, vec) * (1.0 / samples)
    factor = lower_inverse(spread)
    out_ref[...] = math.sqrt(samples) * jnp.dot(
        factor, remainder, precision=HIGHEST, preferred_element_type=F32
    )

    for j in range(1, 16):
        src_copy(j).wait_send()
    for j in range(16):
        sib_copy(j).wait_send()
    for e in near + far:
        tgt_copy(e).wait_send()
    for e in ups:
        part_copy(e).wait_send()

    def wait_sent(k, _):
        ga_copy(k).wait_send()
        gb_copy(k).wait_send()
        return 0

    lax.fori_loop(1, 16, wait_sent, 0)

    def wait_gc_sent(k, _):
        gc_copy(1, k).wait_send()

        @pl.when(k > 0)
        def _():
            gc_copy(0, k).wait_send()

        return 0

    lax.fori_loop(0, 8, wait_gc_sent, 0)


def per_device(descriptors, densities, vectors):
    dma = pltpu.SemaphoreType.DMA
    return pl.pallas_call(
        kernel,
        out_shape=jax.ShapeDtypeStruct((32, BLOCK), F32),
        in_specs=[pl.BlockSpec(memory_space=pltpu.VMEM)] * 3,
        out_specs=pl.BlockSpec(memory_space=pltpu.VMEM),
        scratch_shapes=[
            pltpu.VMEM((2, 16, 160, 128), BF16),
            pltpu.VMEM((16, 48, 128), BF16),
            pltpu.VMEM((2, 12, 128, 256), BF16),
            pltpu.VMEM((16, 48, 384), BF16),
            pltpu.VMEM((12, 48, 256), F32),
            pltpu.VMEM((16, 64, 128), BF16),
            pltpu.VMEM((16, 64, 128), BF16),
            pltpu.VMEM((2, 16, 8, 128), F32),
            pltpu.VMEM((16, 8, 128), F32),
            pltpu.VMEM((2, 8, 8, 128), F32),
            *([dma((16,))] * 12),
            dma((2, 8)), dma((2, 8)),
        ],
        compiler_params=pltpu.CompilerParams(
            collective_id=0, has_side_effects=True, vmem_limit_bytes=48 << 20
        ),
    )(descriptors, densities.reshape(1, BLOCK), vectors)


def solution(mesh):
    placed = P(None, ("row", "col"))
    return jax.shard_map(
        per_device,
        mesh=mesh,
        in_specs=(placed, P(("row", "col")), placed),
        out_specs=placed,
        check_vma=False,
    )
```

```python
import functools
import math

import jax
import jax.numpy as jnp
from jax import lax
from jax.experimental import pallas as pl
from jax.experimental.pallas import tpu as pltpu
from jax.sharding import PartitionSpec as P

MESH = pl.DeviceIdType.MESH
HIGHEST = lax.Precision.HIGHEST
F32, BF16 = jnp.float32, jnp.bfloat16

BLOCK = 192
PLANE = 16
DEPTH = 16
EXPONENT = math.log2(math.e) / 4.0


def norm_rows(x):
    half = 0.5 * jnp.sum(x * x, axis=0, keepdims=True)
    rest = jnp.broadcast_to(half, (16, half.shape[1]))
    at = lax.broadcasted_iota(jnp.int32, rest.shape, 0)
    rows = jnp.zeros_like(rest)
    for k in range(3):
        piece = rest.astype(BF16).astype(F32)
        rest = rest - piece
        rows = jnp.where(at == k, -piece, rows)
    return rows


def unit_rows(width):
    at = lax.broadcasted_iota(jnp.int32, (16, width), 0)
    return jnp.where(at < 3, 1.0, 0.0)


def lower_inverse(spread):
    n = spread.shape[0]
    at_row = lax.broadcasted_iota(jnp.int32, (n, 2 * n), 0)
    at_col = lax.broadcasted_iota(jnp.int32, (n, 2 * n), 1)
    both = jnp.concatenate([spread, spread], axis=1)
    work = jnp.where(at_col < n, both, jnp.where(at_col - n == at_row, 1.0, 0.0))
    for k in range(n):
        pivot_row = work[k : k + 1, :]
        inverse = lax.rsqrt(work[k : k + 1, k : k + 1])
        pivot_row = pivot_row * inverse
        column = work[:, k : k + 1] * inverse
        work = jnp.where(
            at_row > k, work - column * pivot_row, jnp.where(at_row == k, pivot_row, work)
        )
    return work[:, n:]


NEAR = sorted(
    ((dx, dy) for dx in range(4) for dy in range(4)),
    key=lambda o: min(o[0], 4 - o[0]) + min(o[1], 4 - o[1]),
)
PAIRS = ((4, -3), (3, -2), (8, -7), (7, -6), (6, -5), (5, -4), (2, -1), (1, 0))
REACH = 4


def kernel(
    desc_hbm, dens_hbm, vec_hbm, out_ref,
    desc_ref, dens_ref, vec_ref, src, feats, tgt, wts, acc, parts_out, parts_in,
    basis_out, basis_plane, basis_z, basis_sib, gram_out, gram_plane, gram_z, gram_sib,
    in_s, src_s, src_r, sib_s, sib_r, tgt_s, tgt_r, part_s, part_r,
    bp_s, bp_r, bz_s, bz_r, gp_s, gp_r, gz_s, gz_r, one_s, one_r,
):
    loads = [
        pltpu.make_async_copy(there, here, in_s.at[k])
        for k, (there, here) in enumerate(
            ((desc_hbm, desc_ref), (dens_hbm, dens_ref), (vec_hbm, vec_ref))
        )
    ]
    for load in loads:
        load.start()
    row, z = lax.axis_index("row"), lax.axis_index("col")
    p, c = row // 2, row % 2
    px, py = p // 4, p % 4
    other = 1 - c
    samples = float(BLOCK * PLANE * DEPTH * 2)

    def chip(dx, dy):
        return ((px + dx) % 4) * 4 + (py + dy) % 4

    def along(d):
        return (z + d + DEPTH) % DEPTH

    barrier = pltpu.get_barrier_semaphore()

    def greet(device):
        pl.semaphore_signal(barrier, inc=1, device_id=device, device_id_type=MESH)

    for d in range(1, REACH + 1):
        greet((row, along(d)))
        greet((row, along(-d)))
    for dx, dy in NEAR[1:]:
        greet((chip(dx, dy) * 2 + c, z))
    greet((p * 2 + other, z))

    lane16 = lax.broadcasted_iota(jnp.int32, (16, 128), 1)
    at16 = lax.broadcasted_iota(jnp.int32, (16, 128), 0)
    turn = lambda v: pltpu.roll(v, 64, 1)
    pad = lambda v: jnp.concatenate([v, jnp.zeros((v.shape[0], 256 - BLOCK), v.dtype)], axis=1)

    def fold(v):
        return jnp.where(lane16 < 64, v[:16], turn(v[16:]))

    def merge(first, second):
        return jnp.concatenate(
            [jnp.where(lane16 < 64, first, turn(second)), jnp.where(lane16 < 64, turn(first), second)],
            axis=0,
        )

    for load in loads:
        load.wait()
    def wide(v):
        return jnp.concatenate([v[8 * g : 8 * g + 8] for g in range(4)], axis=1)

    def square(v):
        return jnp.concatenate([v[:, 32 * g : 32 * g + 32] for g in range(4)], axis=0)

    x = pad(desc_ref[...].astype(F32))
    feats[7, 0:32] = x[:, :128].astype(BF16)
    feats[7, 32:48] = fold(x[:, 128:]).astype(BF16)
    source = jnp.concatenate([x, norm_rows(x), unit_rows(256)], axis=0)
    later = pltpu.roll(source, 160, 1)
    packed = jnp.concatenate([source[:, :128], later[:, :128]], axis=0).T[:96]
    src[0, 0, 0:96] = packed.astype(BF16)
    vec = vec_ref[...]
    inverse = pad(1.0 / dens_ref[...])
    weighted = pad(vec / dens_ref[...])
    src[0, 0, 96:128] = weighted[:, :128].astype(BF16)
    src[0, 0, 128:144] = fold(weighted[:, 128:]).astype(BF16)
    tail = jnp.broadcast_to(inverse[:, 128:], (16, 128))
    src[0, 0, 144:160] = jnp.where(
        at16 == 0,
        jnp.broadcast_to(inverse[:, :128], (16, 128)),
        jnp.where(at16 == 1, jnp.where(lane16 < 64, tail, turn(tail)), 0.0),
    ).astype(BF16)

    basis_out[0] = wide(
        lax.dot_general(
            vec, vec, (((1,), (1,)), ((), ())), precision=HIGHEST, preferred_element_type=F32
        )
    )
    pl.semaphore_wait(barrier, 2 * REACH + 16)

    def remote(source_ref, target_ref, send_sem, recv_sem, device):
        return pltpu.make_async_remote_copy(
            src_ref=source_ref, dst_ref=target_ref, send_sem=send_sem, recv_sem=recv_sem,
            device_id=device, device_id_type=MESH,
        )

    def src_copy(j):
        return remote(
            src.at[0, 0], src.at[0, j], src_s.at[j], src_r.at[j], (chip(*NEAR[j]) * 2 + c, z)
        )

    def sib_copy(j):
        return remote(
            src.at[0, j], src.at[1, j], sib_s.at[j], sib_r.at[j], (p * 2 + other, z)
        )

    def tgt_copy(e):
        if abs(e) <= REACH:
            return remote(
                feats.at[7], feats.at[7 + e], tgt_s.at[7 + e], tgt_r.at[7 + e], (row, along(-e))
            )
        step = REACH if e > 0 else -REACH
        return remote(
            feats.at[7 + e - step], feats.at[7 + e], tgt_s.at[7 + e], tgt_r.at[7 + e],
            (row, along(-step)),
        )

    def plane_copy(here, there, sends, receives, j):
        return remote(
            here.at[0], there.at[j], sends.at[j], receives.at[j], (chip(*NEAR[j]) * 2 + c, z)
        )

    def z_copy(here, there, sends, receives, k):
        return remote(here.at[1], there.at[k], sends.at[k], receives.at[k], (row, along(k)))

    def sib_one(here, there, k):
        return remote(here, there, one_s.at[k], one_r.at[k], (p * 2 + other, z))

    basis_p = functools.partial(plane_copy, basis_out, basis_plane, bp_s, bp_r)
    basis_a = functools.partial(z_copy, basis_out, basis_z, bz_s, bz_r)
    gram_p = functools.partial(plane_copy, gram_out, gram_plane, gp_s, gp_r)
    gram_a = functools.partial(z_copy, gram_out, gram_z, gz_s, gz_r)

    def collect(copy, own, slots):
        total = own
        for k in range(1, 16):
            copy(k).wait_recv()
            total = total + slots[k]
        return total

    near = [e for d in range(1, REACH + 1) for e in (d, -d)]
    far = [e for d in range(1, REACH + 1) for e in (d + REACH, -d - REACH) if e > -8]
    for e in near:
        tgt_copy(e).start()
    sib_copy(0).start()
    for j in range(1, 16):
        src_copy(j).start()
    for j in range(1, 16):
        basis_p(j).start()
    acc[...] = jnp.zeros_like(acc)
    for e in near:
        tgt_copy(e).wait_recv()
        ahead = e + (REACH if e > 0 else -REACH)
        if ahead in far:
            tgt_copy(ahead).start()

    unit_tile = unit_rows(128)
    zeros = jnp.zeros((64, 128), F32)

    def build(pair):
        first, second = (feats[7 + e].astype(F32) for e in PAIRS[pair])
        for t, tile in enumerate((first[:32], second[:32], merge(first[32:], second[32:]))):
            rows = jnp.concatenate([tile, unit_tile, norm_rows(tile)], axis=0)
            k = 3 * pair + t
            at = slice(128 * (k % 2), 128 * (k % 2) + 128)
            tgt[0, k // 2, :, at] = jnp.concatenate([rows, zeros], axis=0).astype(BF16)
            tgt[1, k // 2, :, at] = jnp.concatenate([zeros, rows], axis=0).astype(BF16)

    for pair in range(2):
        build(pair)

    def columns(j):
        first, second = src[0, j], src[1, j]
        wts[j, :, 0:128] = jnp.concatenate([first[96:128], first[144:160]], axis=0)
        wts[j, :, 128:256] = jnp.concatenate([second[96:128], second[144:160]], axis=0)
        tails = merge(first[128:144].astype(F32), second[128:144].astype(F32))
        ends = jnp.where(
            lane16 < 64, first[144:160].astype(F32), second[144:160].astype(F32)
        )
        ends = jnp.where(at16 == 0, jnp.broadcast_to(ends[1:2], (16, 128)), 0.0)
        wts[j, :, 256:384] = jnp.concatenate([tails, ends], axis=0).astype(BF16)

    def work(first_chunk, first_chip, pairs):
        units = [(k, n) for k in range(3) for n in range(pairs)]
        inner, kernels = {}, {}
        for i in range(len(units) + 2):
            if i < len(units):
                k, n = units[i]
                rows = jnp.concatenate(
                    [src[s, first_chip + 2 * n + j, 0:96] for j in range(2) for s in range(2)], axis=0
                )
                inner[i] = [
                    jnp.dot(rows, tgt[v, first_chunk + k], preferred_element_type=F32)
                    for v in range(2)
                ]
            if 0 <= i - 1 < len(units):
                low, high = (
                    jnp.exp2(u * F32(EXPONENT)).astype(BF16) for u in inner.pop(i - 1)
                )
                order = []
                for j in range(2):
                    a, b = 192 * j, 192 * j + 96
                    order += [
                        low[a : a + 96], high[a : a + 32], low[b : b + 96], high[b : b + 32],
                        high[a + 32 : a + 96], high[b + 32 : b + 96],
                    ]
                kernels[i - 1] = jnp.concatenate(order, axis=0)
            if 0 <= i - 2 < len(units):
                k, n = units[i - 2]
                weights = jnp.concatenate(
                    [wts[first_chip + 2 * n + j] for j in range(2)], axis=1
                )
                acc[first_chunk + k] += jnp.dot(
                    weights, kernels.pop(i - 2), preferred_element_type=F32
                )

    def part_copy(e):
        return remote(
            parts_out.at[7 + e], parts_in.at[7 + e], part_s.at[7 + e], part_r.at[7 + e],
            (row, along(e)),
        )

    def send_parts(pair):
        tiles = [
            acc[k // 2, :, 128 * (k % 2) : 128 * (k % 2) + 128]
            for k in range(3 * pair, 3 * pair + 3)
        ]
        both = tiles[2]
        for s, e in enumerate(PAIRS[pair]):
            tail = turn(both) if s else both
            parts_out[7 + e, 0:32] = tiles[s][:32].astype(BF16)
            parts_out[7 + e, 32:48] = fold(tail[:32]).astype(BF16)
            parts_out[7 + e, 48:64] = jnp.where(
                at16 == 0,
                jnp.broadcast_to(tiles[s][32:33], (16, 128)),
                jnp.broadcast_to(tail[32:33], (16, 128)),
            ).astype(BF16)
            if e != 0:
                part_copy(e).start()

    def arrive(m):
        for j in range(4 * m, 4 * m + 4):
            if j > 0:
                src_copy(j).wait_recv()
                sib_copy(j).start()

    arrive(0)
    for m in range(4):
        if m < 3:
            arrive(m + 1)
        for j in range(4 * m, 4 * m + 4):
            sib_copy(j).wait_recv()
            columns(j)
        work(0, 4 * m, 2)
    for pair in range(2):
        send_parts(pair)
    for e in far:
        tgt_copy(e).wait_recv()
    basis_out[1] = collect(basis_p, basis_out[0], basis_plane)
    for k in range(1, 16):
        basis_a(k).start()
    for group in range(1, 4):
        for pair in (2 * group, 2 * group + 1):
            build(pair)

        def rest(m, _):
            work(3 * group, 8 * m, 4)
            return 0

        lax.fori_loop(0, 2, rest, 0)
        for pair in (2 * group, 2 * group + 1):
            send_parts(pair)
        if group == 2:
            basis_out[2] = collect(basis_a, basis_out[1], basis_z)
            sib_one(basis_out.at[2], basis_sib, 0).start()
    sums = parts_out[7].astype(F32)
    ups = [e for pair in PAIRS for e in pair if e != 0]
    for e in ups:
        part_copy(e).wait_recv()
        sums = sums + parts_in[7 + e].astype(F32)
    tail = sums[32:48]
    tail = jnp.concatenate([tail, turn(tail)], axis=0)
    top = jnp.concatenate([sums[:32], tail], axis=1)[:, :BLOCK]
    degree = jnp.concatenate([sums[48:49], sums[49:50]], axis=1)[:, :BLOCK]
    diffused = top / degree

    dot_c = lambda a, b: lax.dot_general(
        a, b, (((1,), (1,)), ((), ())), precision=HIGHEST, preferred_element_type=F32
    )
    grams = (wide(dot_c(vec, diffused)), wide(dot_c(diffused, diffused)))
    first = c == 0
    gram_out[3] = jnp.where(first, grams[1], grams[0])
    swap = sib_one(gram_out.at[3], gram_sib.at[0], 1)
    swap.start()
    swap.wait_recv()
    gram_out[0] = jnp.where(first, grams[0], grams[1]) + gram_sib[0]
    for k in range(1, 16):
        gram_p(k).start()
    gram_out[1] = collect(gram_p, gram_out[0], gram_plane)
    for k in range(1, 16):
        gram_a(k).start()
    sib_one(basis_out.at[2], basis_sib, 0).wait_recv()
    basis = square(basis_out[2] + basis_sib[...])
    gram_out[2] = collect(gram_a, gram_out[1], gram_z)
    swap_back = sib_one(gram_out.at[2], gram_sib.at[1], 2)
    swap_back.start()
    swap_back.wait_recv()
    mine, others = gram_out[2], gram_sib[1]
    coupling = square(jnp.where(first, mine, others))
    diffused_gram = square(jnp.where(first, others, mine))
    dot_t = lambda a, b: lax.dot_general(
        a, b, (((0,), (0,)), ((), ())), precision=HIGHEST, preferred_element_type=F32
    )
    mixed = jnp.dot(basis, coupling, precision=HIGHEST, preferred_element_type=F32)
    spread = diffused_gram + dot_t(
        coupling, mixed * (1.0 / (samples * samples)) - coupling * (2.0 / samples)
    )
    remainder = diffused - dot_t(coupling, vec) * (1.0 / samples)
    factor = lower_inverse(spread)
    out_ref[...] = math.sqrt(samples) * jnp.dot(
        factor, remainder, precision=HIGHEST, preferred_element_type=F32
    )

    for j in range(1, 16):
        src_copy(j).wait_send()
    for j in range(16):
        sib_copy(j).wait_send()
    for e in near + far:
        tgt_copy(e).wait_send()
    for e in ups:
        part_copy(e).wait_send()

    for k in range(1, 16):
        for copy in (basis_p, basis_a, gram_p, gram_a):
            copy(k).wait_send()
    sib_one(basis_out.at[2], basis_sib, 0).wait_send()
    swap.wait_send()
    swap_back.wait_send()


def per_device(descriptors, densities, vectors):
    dma = pltpu.SemaphoreType.DMA
    return pl.pallas_call(
        kernel,
        out_shape=jax.ShapeDtypeStruct((32, BLOCK), F32),
        in_specs=[pl.BlockSpec(memory_space=pl.ANY)] * 3,
        out_specs=pl.BlockSpec(memory_space=pltpu.VMEM),
        scratch_shapes=[
            pltpu.VMEM((32, BLOCK), BF16),
            pltpu.VMEM((1, BLOCK), F32),
            pltpu.VMEM((32, BLOCK), F32),
            pltpu.VMEM((2, 16, 160, 128), BF16),
            pltpu.VMEM((16, 48, 128), BF16),
            pltpu.VMEM((2, 12, 128, 256), BF16),
            pltpu.VMEM((16, 48, 384), BF16),
            pltpu.VMEM((12, 48, 256), F32),
            pltpu.VMEM((16, 64, 128), BF16),
            pltpu.VMEM((16, 64, 128), BF16),
            pltpu.VMEM((3, 8, 128), F32),
            pltpu.VMEM((16, 8, 128), F32),
            pltpu.VMEM((16, 8, 128), F32),
            pltpu.VMEM((8, 128), F32),
            pltpu.VMEM((4, 8, 128), F32),
            pltpu.VMEM((16, 8, 128), F32),
            pltpu.VMEM((16, 8, 128), F32),
            pltpu.VMEM((2, 8, 128), F32),
            dma((3,)),
            *([dma((16,))] * 16),
            dma((3,)), dma((3,)),
        ],
        compiler_params=pltpu.CompilerParams(
            collective_id=0, has_side_effects=True, vmem_limit_bytes=63 << 20
        ),
    )(descriptors, densities.reshape(1, BLOCK), vectors)


def solution(mesh):
    placed = P(None, ("row", "col"))
    return jax.shard_map(
        per_device,
        mesh=mesh,
        in_specs=(placed, P(("row", "col")), placed),
        out_specs=placed,
        check_vma=False,
    )
```

```python
import functools
import math

import jax
import jax.numpy as jnp
from jax import lax
from jax.experimental import pallas as pl
from jax.experimental.pallas import tpu as pltpu
from jax.sharding import PartitionSpec as P

MESH = pl.DeviceIdType.MESH
HIGHEST = lax.Precision.HIGHEST
F32, BF16 = jnp.float32, jnp.bfloat16

BLOCK = 192
PLANE = 16
DEPTH = 16
EXPONENT = math.log2(math.e) / 4.0


def norm_rows(x):
    half = 0.5 * jnp.sum(x * x, axis=0, keepdims=True)
    rest = jnp.broadcast_to(half, (16, half.shape[1]))
    at = lax.broadcasted_iota(jnp.int32, rest.shape, 0)
    rows = jnp.zeros_like(rest)
    for k in range(3):
        piece = rest.astype(BF16).astype(F32)
        rest = rest - piece
        rows = jnp.where(at == k, -piece, rows)
    return rows


def unit_rows(width):
    at = lax.broadcasted_iota(jnp.int32, (16, width), 0)
    return jnp.where(at < 3, 1.0, 0.0)


def lower_inverse(spread):
    n, step = spread.shape[0], 4
    shape = (n, 2 * n)
    at_row = lax.broadcasted_iota(jnp.int32, shape, 0)
    at_col = lax.broadcasted_iota(jnp.int32, shape, 1)
    both = jnp.concatenate([spread, spread], axis=1)
    work = jnp.where(at_col < n, both, jnp.where(at_col - n == at_row, 1.0, 0.0))
    finished = []
    for k in range(0, n, step):
        rows = [work[k + i : k + i + 1] for i in range(step)]
        columns = [jnp.broadcast_to(work[:, k + i : k + i + 1], shape) for i in range(step)]
        for i in range(step):
            pivot = columns[i][k + i : k + i + 1]
            finished.append(rows[i] * lax.rsqrt(pivot))
            share = columns[i] * (1.0 / pivot)
            for j in range(i + 1, step):
                rows[j] = rows[j] - share[k + j : k + j + 1] * rows[i]
                columns[j] = columns[j] - share * columns[i][k + j : k + j + 1]
            work = work - share * rows[i]
    return jnp.concatenate(finished, axis=0)[:, n:]


NEAR = sorted(
    ((dx, dy) for dx in range(4) for dy in range(4)),
    key=lambda o: min(o[0], 4 - o[0]) + min(o[1], 4 - o[1]),
)
PAIRS = ((4, -3), (3, -2), (8, -7), (7, -6), (6, -5), (5, -4), (2, -1), (1, 0))
REACH = 4


def kernel(
    desc_hbm, dens_hbm, vec_hbm, out_ref,
    desc_ref, dens_ref, vec_ref, src, feats, tgt, wts, acc, parts_out, parts_in,
    basis_out, basis_plane, basis_z, basis_sib, gram_out, gram_plane, gram_z, gram_sib,
    in_s, src_s, src_r, sib_s, sib_r, tgt_s, tgt_r, part_s, part_r,
    bp_s, bp_r, bz_s, bz_r, gp_s, gp_r, gz_s, gz_r, one_s, one_r,
):
    loads = [
        pltpu.make_async_copy(there, here, in_s.at[k])
        for k, (there, here) in enumerate(
            ((desc_hbm, desc_ref), (dens_hbm, dens_ref), (vec_hbm, vec_ref))
        )
    ]
    for load in loads:
        load.start()
    row, z = lax.axis_index("row"), lax.axis_index("col")
    p, c = row // 2, row % 2
    px, py = p // 4, p % 4
    other = 1 - c
    samples = float(BLOCK * PLANE * DEPTH * 2)

    def chip(dx, dy):
        return ((px + dx) % 4) * 4 + (py + dy) % 4

    def along(d):
        return (z + d + DEPTH) % DEPTH

    barrier = pltpu.get_barrier_semaphore()

    def greet(device):
        pl.semaphore_signal(barrier, inc=1, device_id=device, device_id_type=MESH)

    for d in range(1, REACH + 1):
        greet((row, along(d)))
        greet((row, along(-d)))
    for dx, dy in NEAR[1:]:
        greet((chip(dx, dy) * 2 + c, z))
    greet((p * 2 + other, z))

    lane16 = lax.broadcasted_iota(jnp.int32, (16, 128), 1)
    at16 = lax.broadcasted_iota(jnp.int32, (16, 128), 0)
    turn = lambda v: pltpu.roll(v, 64, 1)
    pad = lambda v: jnp.concatenate([v, jnp.zeros((v.shape[0], 256 - BLOCK), v.dtype)], axis=1)

    def fold(v):
        return jnp.where(lane16 < 64, v[:16], turn(v[16:]))

    def merge(first, second):
        return jnp.concatenate(
            [jnp.where(lane16 < 64, first, turn(second)), jnp.where(lane16 < 64, turn(first), second)],
            axis=0,
        )

    for load in loads:
        load.wait()
    def wide(v):
        return jnp.concatenate([v[8 * g : 8 * g + 8] for g in range(4)], axis=1)

    def square(v):
        return jnp.concatenate([v[:, 32 * g : 32 * g + 32] for g in range(4)], axis=0)

    x = pad(desc_ref[...].astype(F32))
    feats[7, 0:32] = x[:, :128].astype(BF16)
    feats[7, 32:48] = fold(x[:, 128:]).astype(BF16)
    source = jnp.concatenate([x, norm_rows(x), unit_rows(256)], axis=0)
    later = pltpu.roll(source, 160, 1)
    packed = jnp.concatenate([source[:, :128], later[:, :128]], axis=0).T[:96]
    src[0, 0, 0:96] = packed.astype(BF16)
    vec = vec_ref[...]
    inverse = pad(1.0 / dens_ref[...])
    weighted = pad(vec / dens_ref[...])
    src[0, 0, 96:128] = weighted[:, :128].astype(BF16)
    src[0, 0, 128:144] = fold(weighted[:, 128:]).astype(BF16)
    tail = jnp.broadcast_to(inverse[:, 128:], (16, 128))
    src[0, 0, 144:160] = jnp.where(
        at16 == 0,
        jnp.broadcast_to(inverse[:, :128], (16, 128)),
        jnp.where(at16 == 1, jnp.where(lane16 < 64, tail, turn(tail)), 0.0),
    ).astype(BF16)

    basis_out[0] = wide(
        lax.dot_general(
            vec, vec, (((1,), (1,)), ((), ())), precision=HIGHEST, preferred_element_type=F32
        )
    )
    pl.semaphore_wait(barrier, 2 * REACH + 16)

    def remote(source_ref, target_ref, send_sem, recv_sem, device):
        return pltpu.make_async_remote_copy(
            src_ref=source_ref, dst_ref=target_ref, send_sem=send_sem, recv_sem=recv_sem,
            device_id=device, device_id_type=MESH,
        )

    def src_copy(j):
        return remote(
            src.at[0, 0], src.at[0, j], src_s.at[j], src_r.at[j], (chip(*NEAR[j]) * 2 + c, z)
        )

    def sib_copy(j):
        return remote(
            src.at[0, j], src.at[1, j], sib_s.at[j], sib_r.at[j], (p * 2 + other, z)
        )

    def tgt_copy(e):
        if abs(e) <= REACH:
            return remote(
                feats.at[7], feats.at[7 + e], tgt_s.at[7 + e], tgt_r.at[7 + e], (row, along(-e))
            )
        step = REACH if e > 0 else -REACH
        return remote(
            feats.at[7 + e - step], feats.at[7 + e], tgt_s.at[7 + e], tgt_r.at[7 + e],
            (row, along(-step)),
        )

    def plane_copy(here, there, sends, receives, j):
        return remote(
            here.at[0], there.at[j], sends.at[j], receives.at[j], (chip(*NEAR[j]) * 2 + c, z)
        )

    def z_copy(here, there, sends, receives, k):
        return remote(here.at[1], there.at[k], sends.at[k], receives.at[k], (row, along(k)))

    def sib_one(here, there, k):
        return remote(here, there, one_s.at[k], one_r.at[k], (p * 2 + other, z))

    basis_p = functools.partial(plane_copy, basis_out, basis_plane, bp_s, bp_r)
    basis_a = functools.partial(z_copy, basis_out, basis_z, bz_s, bz_r)
    gram_p = functools.partial(plane_copy, gram_out, gram_plane, gp_s, gp_r)
    gram_a = functools.partial(z_copy, gram_out, gram_z, gz_s, gz_r)

    def collect(copy, own, slots):
        total = own
        for k in range(1, 16):
            copy(k).wait_recv()
            total = total + slots[k]
        return total

    near = [e for d in range(1, REACH + 1) for e in (d, -d)]
    far = [e for d in range(1, REACH + 1) for e in (d + REACH, -d - REACH) if e > -8]
    for e in near:
        tgt_copy(e).start()
    sib_copy(0).start()
    for j in range(1, 16):
        src_copy(j).start()
    acc[...] = jnp.zeros_like(acc)
    for e in near:
        tgt_copy(e).wait_recv()
        ahead = e + (REACH if e > 0 else -REACH)
        if ahead in far:
            tgt_copy(ahead).start()

    unit_tile = unit_rows(128)
    zeros = jnp.zeros((64, 128), F32)

    def build(pair):
        first, second = (feats[7 + e].astype(F32) for e in PAIRS[pair])
        for t, tile in enumerate((first[:32], second[:32], merge(first[32:], second[32:]))):
            rows = jnp.concatenate([tile, unit_tile, norm_rows(tile)], axis=0)
            k = 3 * pair + t
            at = slice(128 * (k % 2), 128 * (k % 2) + 128)
            tgt[0, k // 2, :, at] = jnp.concatenate([rows, zeros], axis=0).astype(BF16)
            tgt[1, k // 2, :, at] = jnp.concatenate([zeros, rows], axis=0).astype(BF16)

    for pair in range(2):
        build(pair)

    def columns(j):
        first, second = src[0, j], src[1, j]
        wts[j, :, 0:128] = jnp.concatenate([first[96:128], first[144:160]], axis=0)
        wts[j, :, 128:256] = jnp.concatenate([second[96:128], second[144:160]], axis=0)
        tails = merge(first[128:144].astype(F32), second[128:144].astype(F32))
        ends = jnp.where(
            lane16 < 64, first[144:160].astype(F32), second[144:160].astype(F32)
        )
        ends = jnp.where(at16 == 0, jnp.broadcast_to(ends[1:2], (16, 128)), 0.0)
        wts[j, :, 256:384] = jnp.concatenate([tails, ends], axis=0).astype(BF16)

    def work(first_chunk, first_chip, pairs):
        units = [(k, n) for k in range(3) for n in range(pairs)]
        inner, kernels = {}, {}
        for i in range(len(units) + 2):
            if i < len(units):
                k, n = units[i]
                rows = jnp.concatenate(
                    [src[s, first_chip + 2 * n + j, 0:96] for j in range(2) for s in range(2)], axis=0
                )
                inner[i] = [
                    jnp.dot(rows, tgt[v, first_chunk + k], preferred_element_type=F32)
                    for v in range(2)
                ]
            if 0 <= i - 1 < len(units):
                low, high = (
                    jnp.exp2(u * F32(EXPONENT)).astype(BF16) for u in inner.pop(i - 1)
                )
                order = []
                for j in range(2):
                    a, b = 192 * j, 192 * j + 96
                    order += [
                        low[a : a + 96], high[a : a + 32], low[b : b + 96], high[b : b + 32],
                        high[a + 32 : a + 96], high[b + 32 : b + 96],
                    ]
                kernels[i - 1] = jnp.concatenate(order, axis=0)
            if 0 <= i - 2 < len(units):
                k, n = units[i - 2]
                weights = jnp.concatenate(
                    [wts[first_chip + 2 * n + j] for j in range(2)], axis=1
                )
                acc[first_chunk + k] += jnp.dot(
                    weights, kernels.pop(i - 2), preferred_element_type=F32
                )

    def part_copy(e):
        return remote(
            parts_out.at[7 + e], parts_in.at[7 + e], part_s.at[7 + e], part_r.at[7 + e],
            (row, along(e)),
        )

    def send_parts(pair):
        tiles = [
            acc[k // 2, :, 128 * (k % 2) : 128 * (k % 2) + 128]
            for k in range(3 * pair, 3 * pair + 3)
        ]
        both = tiles[2]
        for s, e in enumerate(PAIRS[pair]):
            tail = turn(both) if s else both
            parts_out[7 + e, 0:32] = tiles[s][:32].astype(BF16)
            parts_out[7 + e, 32:48] = fold(tail[:32]).astype(BF16)
            parts_out[7 + e, 48:64] = jnp.where(
                at16 == 0,
                jnp.broadcast_to(tiles[s][32:33], (16, 128)),
                jnp.broadcast_to(tail[32:33], (16, 128)),
            ).astype(BF16)
            if e != 0:
                part_copy(e).start()

    def arrive(m):
        for j in range(4 * m, 4 * m + 4):
            if j > 0:
                src_copy(j).wait_recv()
                sib_copy(j).start()

    arrive(0)
    for m in range(4):
        if m < 3:
            arrive(m + 1)
        for j in range(4 * m, 4 * m + 4):
            sib_copy(j).wait_recv()
            columns(j)
        if m == 3:
            for j in range(1, 16):
                basis_p(j).start()
        work(0, 4 * m, 2)
    for pair in range(2):
        send_parts(pair)
    for e in far:
        tgt_copy(e).wait_recv()
    for group in range(1, 4):
        for pair in (2 * group, 2 * group + 1):
            build(pair)

        def rest(m, _):
            work(3 * group, 8 * m, 4)
            return 0

        lax.fori_loop(0, 2, rest, 0)
        for pair in (2 * group, 2 * group + 1):
            send_parts(pair)
        if group == 1:
            basis_out[1] = collect(basis_p, basis_out[0], basis_plane)
            for k in range(1, 16):
                basis_a(k).start()
    sums = parts_out[7].astype(F32)
    ups = [e for pair in PAIRS for e in pair if e != 0]
    for e in ups:
        part_copy(e).wait_recv()
        sums = sums + parts_in[7 + e].astype(F32)
    tail = sums[32:48]
    tail = jnp.concatenate([tail, turn(tail)], axis=0)
    top = jnp.concatenate([sums[:32], tail], axis=1)[:, :BLOCK]
    degree = jnp.concatenate([sums[48:49], sums[49:50]], axis=1)[:, :BLOCK]
    diffused = top / degree

    dot_c = lambda a, b: lax.dot_general(
        a, b, (((1,), (1,)), ((), ())), precision=HIGHEST, preferred_element_type=F32
    )
    grams = (wide(dot_c(vec, diffused)), wide(dot_c(diffused, diffused)))
    first = c == 0
    gram_out[3] = jnp.where(first, grams[1], grams[0])
    swap = sib_one(gram_out.at[3], gram_sib.at[0], 1)
    swap.start()
    swap.wait_recv()
    gram_out[0] = jnp.where(first, grams[0], grams[1]) + gram_sib[0]
    for k in range(15, 0, -1):
        gram_p(k).start()
    basis_out[2] = collect(basis_a, basis_out[1], basis_z)
    sib_one(basis_out.at[2], basis_sib, 0).start()
    gram_out[1] = collect(gram_p, gram_out[0], gram_plane)
    for k in sorted(range(1, 16), key=lambda k: -min(k, DEPTH - k)):
        gram_a(k).start()
    sib_one(basis_out.at[2], basis_sib, 0).wait_recv()
    basis = square(basis_out[2] + basis_sib[...])
    gram_out[2] = collect(gram_a, gram_out[1], gram_z)
    swap_back = sib_one(gram_out.at[2], gram_sib.at[1], 2)
    swap_back.start()
    swap_back.wait_recv()
    mine, others = gram_out[2], gram_sib[1]
    coupling = square(jnp.where(first, mine, others))
    diffused_gram = square(jnp.where(first, others, mine))
    dot_t = lambda a, b: lax.dot_general(
        a, b, (((0,), (0,)), ((), ())), precision=HIGHEST, preferred_element_type=F32
    )
    mixed = jnp.dot(basis, coupling, precision=HIGHEST, preferred_element_type=F32)
    spread = diffused_gram + dot_t(
        coupling, mixed * (1.0 / (samples * samples)) - coupling * (2.0 / samples)
    )
    remainder = diffused - dot_t(coupling, vec) * (1.0 / samples)
    factor = lower_inverse(spread)
    out_ref[...] = math.sqrt(samples) * jnp.dot(
        factor, remainder, precision=HIGHEST, preferred_element_type=F32
    )

    for j in range(1, 16):
        src_copy(j).wait_send()
    for j in range(16):
        sib_copy(j).wait_send()
    for e in near + far:
        tgt_copy(e).wait_send()
    for e in ups:
        part_copy(e).wait_send()

    for k in range(1, 16):
        for copy in (basis_p, basis_a, gram_p, gram_a):
            copy(k).wait_send()
    sib_one(basis_out.at[2], basis_sib, 0).wait_send()
    swap.wait_send()
    swap_back.wait_send()


def per_device(descriptors, densities, vectors):
    dma = pltpu.SemaphoreType.DMA
    return pl.pallas_call(
        kernel,
        out_shape=jax.ShapeDtypeStruct((32, BLOCK), F32),
        in_specs=[pl.BlockSpec(memory_space=pl.ANY)] * 3,
        out_specs=pl.BlockSpec(memory_space=pltpu.VMEM),
        scratch_shapes=[
            pltpu.VMEM((32, BLOCK), BF16),
            pltpu.VMEM((1, BLOCK), F32),
            pltpu.VMEM((32, BLOCK), F32),
            pltpu.VMEM((2, 16, 160, 128), BF16),
            pltpu.VMEM((16, 48, 128), BF16),
            pltpu.VMEM((2, 12, 128, 256), BF16),
            pltpu.VMEM((16, 48, 384), BF16),
            pltpu.VMEM((12, 48, 256), F32),
            pltpu.VMEM((16, 64, 128), BF16),
            pltpu.VMEM((16, 64, 128), BF16),
            pltpu.VMEM((3, 8, 128), F32),
            pltpu.VMEM((16, 8, 128), F32),
            pltpu.VMEM((16, 8, 128), F32),
            pltpu.VMEM((8, 128), F32),
            pltpu.VMEM((4, 8, 128), F32),
            pltpu.VMEM((16, 8, 128), F32),
            pltpu.VMEM((16, 8, 128), F32),
            pltpu.VMEM((2, 8, 128), F32),
            dma((3,)),
            *([dma((16,))] * 16),
            dma((3,)), dma((3,)),
        ],
        compiler_params=pltpu.CompilerParams(
            collective_id=0, has_side_effects=True, vmem_limit_bytes=63 << 20
        ),
    )(descriptors, densities.reshape(1, BLOCK), vectors)


def solution(mesh):
    placed = P(None, ("row", "col"))
    return jax.shard_map(
        per_device,
        mesh=mesh,
        in_specs=(placed, P(("row", "col")), placed),
        out_specs=placed,
        check_vma=False,
    )
```

```python
import functools
import math

import jax
import jax.numpy as jnp
from jax import lax
from jax.experimental import pallas as pl
from jax.experimental.pallas import tpu as pltpu
from jax.sharding import PartitionSpec as P

MESH = pl.DeviceIdType.MESH
HIGHEST = lax.Precision.HIGHEST
F32, BF16 = jnp.float32, jnp.bfloat16

BLOCK = 192
PLANE = 16
DEPTH = 16
EXPONENT = math.log2(math.e) / 4.0


def norm_rows(x):
    half = 0.5 * jnp.sum(x * x, axis=0, keepdims=True)
    rest = jnp.broadcast_to(half, (16, half.shape[1]))
    at = lax.broadcasted_iota(jnp.int32, rest.shape, 0)
    rows = jnp.zeros_like(rest)
    for k in range(3):
        piece = rest.astype(BF16).astype(F32)
        rest = rest - piece
        rows = jnp.where(at == k, -piece, rows)
    return rows


def unit_rows(width):
    at = lax.broadcasted_iota(jnp.int32, (16, width), 0)
    return jnp.where(at < 3, 1.0, 0.0)


def lower_inverse(spread):
    n, step = spread.shape[0], 4
    shape = (n, 2 * n)
    at_row = lax.broadcasted_iota(jnp.int32, shape, 0)
    at_col = lax.broadcasted_iota(jnp.int32, shape, 1)
    both = jnp.concatenate([spread, spread], axis=1)
    work = jnp.where(at_col < n, both, jnp.where(at_col - n == at_row, 1.0, 0.0))
    finished = []
    for k in range(0, n, step):
        rows = [work[k + i : k + i + 1] for i in range(step)]
        columns = [jnp.broadcast_to(work[:, k + i : k + i + 1], shape) for i in range(step)]
        for i in range(step):
            pivot = columns[i][k + i : k + i + 1]
            finished.append(rows[i] * lax.rsqrt(pivot))
            share = columns[i] * (1.0 / pivot)
            for j in range(i + 1, step):
                rows[j] = rows[j] - share[k + j : k + j + 1] * rows[i]
                columns[j] = columns[j] - share * columns[i][k + j : k + j + 1]
            work = work - share * rows[i]
    return jnp.concatenate(finished, axis=0)[:, n:]


NEAR = sorted(
    ((dx, dy) for dx in range(4) for dy in range(4)),
    key=lambda o: min(o[0], 4 - o[0]) + min(o[1], 4 - o[1]),
)
PAIRS = ((4, -3), (3, -2), (8, -7), (7, -6), (6, -5), (5, -4), (2, -1), (1, 0))
REACH = 4


def kernel(
    desc_hbm, dens_hbm, vec_hbm, out_ref,
    desc_ref, dens_ref, vec_ref, src, feats, tgt, wts, acc, parts_out, parts_in,
    basis_out, basis_plane, basis_z, basis_sib, gram_out, gram_plane, gram_z, gram_sib,
    in_s, src_s, src_r, sib_s, sib_r, tgt_s, tgt_r, part_s, part_r,
    bp_s, bp_r, bz_s, bz_r, gp_s, gp_r, gz_s, gz_r, one_s, one_r,
):
    loads = [
        pltpu.make_async_copy(there, here, in_s.at[k])
        for k, (there, here) in enumerate(
            ((desc_hbm, desc_ref), (dens_hbm, dens_ref), (vec_hbm, vec_ref))
        )
    ]
    for load in loads:
        load.start()
    row, z = lax.axis_index("row"), lax.axis_index("col")
    p, c = row // 2, row % 2
    px, py = p // 4, p % 4
    other = 1 - c
    samples = float(BLOCK * PLANE * DEPTH * 2)

    def chip(dx, dy):
        return ((px + dx) % 4) * 4 + (py + dy) % 4

    def along(d):
        return (z + d + DEPTH) % DEPTH

    barrier = pltpu.get_barrier_semaphore()

    def greet(device):
        pl.semaphore_signal(barrier, inc=1, device_id=device, device_id_type=MESH)

    for d in range(1, REACH + 1):
        greet((row, along(d)))
        greet((row, along(-d)))
    for dx, dy in NEAR[1:]:
        greet((chip(dx, dy) * 2 + c, z))
    greet((p * 2 + other, z))

    lane16 = lax.broadcasted_iota(jnp.int32, (16, 128), 1)
    at16 = lax.broadcasted_iota(jnp.int32, (16, 128), 0)
    turn = lambda v: pltpu.roll(v, 64, 1)
    pad = lambda v: jnp.concatenate([v, jnp.zeros((v.shape[0], 256 - BLOCK), v.dtype)], axis=1)

    def fold(v):
        return jnp.where(lane16 < 64, v[:16], turn(v[16:]))

    def merge(first, second):
        return jnp.concatenate(
            [jnp.where(lane16 < 64, first, turn(second)), jnp.where(lane16 < 64, turn(first), second)],
            axis=0,
        )

    for load in loads:
        load.wait()
    def wide(v):
        return jnp.concatenate([v[8 * g : 8 * g + 8] for g in range(4)], axis=1)

    def square(v):
        return jnp.concatenate([v[:, 32 * g : 32 * g + 32] for g in range(4)], axis=0)

    x = pad(desc_ref[...].astype(F32))
    feats[7, 0:32] = x[:, :128].astype(BF16)
    feats[7, 32:48] = fold(x[:, 128:]).astype(BF16)
    source = jnp.concatenate([x, norm_rows(x), unit_rows(256)], axis=0)
    later = pltpu.roll(source, 160, 1)
    packed = jnp.concatenate([source[:, :128], later[:, :128]], axis=0).T[:96]
    src[0, 0, 0:96] = packed.astype(BF16)
    vec = vec_ref[...]
    inverse = pad(1.0 / dens_ref[...])
    weighted = pad(vec / dens_ref[...])
    src[0, 0, 96:128] = weighted[:, :128].astype(BF16)
    src[0, 0, 128:144] = fold(weighted[:, 128:]).astype(BF16)
    tail = jnp.broadcast_to(inverse[:, 128:], (16, 128))
    src[0, 0, 144:160] = jnp.where(
        at16 == 0,
        jnp.broadcast_to(inverse[:, :128], (16, 128)),
        jnp.where(at16 == 1, jnp.where(lane16 < 64, tail, turn(tail)), 0.0),
    ).astype(BF16)

    basis_out[0] = wide(
        lax.dot_general(
            vec, vec, (((1,), (1,)), ((), ())), precision=HIGHEST, preferred_element_type=F32
        )
    )
    pl.semaphore_wait(barrier, 2 * REACH + 16)

    def remote(source_ref, target_ref, send_sem, recv_sem, device):
        return pltpu.make_async_remote_copy(
            src_ref=source_ref, dst_ref=target_ref, send_sem=send_sem, recv_sem=recv_sem,
            device_id=device, device_id_type=MESH,
        )

    def src_copy(j):
        return remote(
            src.at[0, 0], src.at[0, j], src_s.at[j], src_r.at[j], (chip(*NEAR[j]) * 2 + c, z)
        )

    def sib_copy(j):
        return remote(
            src.at[0, j], src.at[1, j], sib_s.at[j], sib_r.at[j], (p * 2 + other, z)
        )

    def tgt_copy(e):
        if abs(e) <= REACH:
            return remote(
                feats.at[7], feats.at[7 + e], tgt_s.at[7 + e], tgt_r.at[7 + e], (row, along(-e))
            )
        step = REACH if e > 0 else -REACH
        return remote(
            feats.at[7 + e - step], feats.at[7 + e], tgt_s.at[7 + e], tgt_r.at[7 + e],
            (row, along(-step)),
        )

    def plane_copy(here, there, sends, receives, j):
        return remote(
            here.at[0], there.at[j], sends.at[j], receives.at[j], (chip(*NEAR[j]) * 2 + c, z)
        )

    def z_copy(here, there, sends, receives, k):
        return remote(here.at[1], there.at[k], sends.at[k], receives.at[k], (row, along(k)))

    def sib_one(here, there, k):
        return remote(here, there, one_s.at[k], one_r.at[k], (p * 2 + other, z))

    basis_p = functools.partial(plane_copy, basis_out, basis_plane, bp_s, bp_r)
    basis_a = functools.partial(z_copy, basis_out, basis_z, bz_s, bz_r)
    gram_p = functools.partial(plane_copy, gram_out, gram_plane, gp_s, gp_r)
    gram_a = functools.partial(z_copy, gram_out, gram_z, gz_s, gz_r)

    def collect(copy, own, slots):
        total = own
        for k in range(1, 16):
            copy(k).wait_recv()
            total = total + slots[k]
        return total

    near = [e for d in range(1, REACH + 1) for e in (d, -d)]
    far = [e for d in range(1, REACH + 1) for e in (d + REACH, -d - REACH) if e > -8]
    for e in near:
        tgt_copy(e).start()
    sib_copy(0).start()
    for j in range(1, 16):
        src_copy(j).start()
    acc[...] = jnp.zeros_like(acc)
    def arrive(m):
        for j in range(4 * m, 4 * m + 4):
            if j > 0:
                src_copy(j).wait_recv()
                sib_copy(j).start()

    arrive(0)
    for e in near:
        tgt_copy(e).wait_recv()
        ahead = e + (REACH if e > 0 else -REACH)
        if ahead in far:
            tgt_copy(ahead).start()

    unit_tile = unit_rows(128)
    zeros = jnp.zeros((64, 128), F32)

    def build(pair):
        first, second = (feats[7 + e].astype(F32) for e in PAIRS[pair])
        for t, tile in enumerate((first[:32], second[:32], merge(first[32:], second[32:]))):
            rows = jnp.concatenate([tile, unit_tile, norm_rows(tile)], axis=0)
            k = 3 * pair + t
            at = slice(128 * (k % 2), 128 * (k % 2) + 128)
            tgt[0, k // 2, :, at] = jnp.concatenate([rows, zeros], axis=0).astype(BF16)
            tgt[1, k // 2, :, at] = jnp.concatenate([zeros, rows], axis=0).astype(BF16)

    for pair in range(2):
        build(pair)

    def columns(j):
        first, second = src[0, j], src[1, j]
        wts[j, :, 0:128] = jnp.concatenate([first[96:128], first[144:160]], axis=0)
        wts[j, :, 128:256] = jnp.concatenate([second[96:128], second[144:160]], axis=0)
        tails = merge(first[128:144].astype(F32), second[128:144].astype(F32))
        ends = jnp.where(
            lane16 < 64, first[144:160].astype(F32), second[144:160].astype(F32)
        )
        ends = jnp.where(at16 == 0, jnp.broadcast_to(ends[1:2], (16, 128)), 0.0)
        wts[j, :, 256:384] = jnp.concatenate([tails, ends], axis=0).astype(BF16)

    def work(first_chunk, first_chip, pairs, chunks=3):
        units = [(k, n) for k in range(chunks) for n in range(pairs)]
        inner, kernels = {}, {}
        for i in range(len(units) + 2):
            if i < len(units):
                k, n = units[i]
                rows = jnp.concatenate(
                    [src[s, first_chip + 2 * n + j, 0:96] for j in range(2) for s in range(2)], axis=0
                )
                inner[i] = [
                    jnp.dot(rows, tgt[v, first_chunk + k], preferred_element_type=F32)
                    for v in range(2)
                ]
            if 0 <= i - 1 < len(units):
                low, high = (
                    jnp.exp2(u * F32(EXPONENT)).astype(BF16) for u in inner.pop(i - 1)
                )
                order = []
                for j in range(2):
                    a, b = 192 * j, 192 * j + 96
                    order += [
                        low[a : a + 96], high[a : a + 32], low[b : b + 96], high[b : b + 32],
                        high[a + 32 : a + 96], high[b + 32 : b + 96],
                    ]
                kernels[i - 1] = jnp.concatenate(order, axis=0)
            if 0 <= i - 2 < len(units):
                k, n = units[i - 2]
                weights = jnp.concatenate(
                    [wts[first_chip + 2 * n + j] for j in range(2)], axis=1
                )
                acc[first_chunk + k] += jnp.dot(
                    weights, kernels.pop(i - 2), preferred_element_type=F32
                )

    def part_copy(e):
        return remote(
            parts_out.at[7 + e], parts_in.at[7 + e], part_s.at[7 + e], part_r.at[7 + e],
            (row, along(e)),
        )

    def send_parts(pair):
        tiles = [
            acc[k // 2, :, 128 * (k % 2) : 128 * (k % 2) + 128]
            for k in range(3 * pair, 3 * pair + 3)
        ]
        both = tiles[2]
        for s, e in enumerate(PAIRS[pair]):
            tail = turn(both) if s else both
            parts_out[7 + e, 0:32] = tiles[s][:32].astype(BF16)
            parts_out[7 + e, 32:48] = fold(tail[:32]).astype(BF16)
            parts_out[7 + e, 48:64] = jnp.where(
                at16 == 0,
                jnp.broadcast_to(tiles[s][32:33], (16, 128)),
                jnp.broadcast_to(tail[32:33], (16, 128)),
            ).astype(BF16)
            if e != 0:
                part_copy(e).start()

    for m in range(4):
        if m < 3:
            arrive(m + 1)
        for j in range(4 * m, 4 * m + 4):
            sib_copy(j).wait_recv()
            columns(j)
        if m == 3:
            for j in range(1, 16):
                basis_p(j).start()
        work(0, 4 * m, 2)
    for pair in range(2):
        send_parts(pair)
    for e in far:
        tgt_copy(e).wait_recv()
    for group in range(1, 4):
        for pair in (2 * group, 2 * group + 1):
            build(pair)

        def rest(m, _):
            work(3 * group, 8 * m, 4, 2 if group == 3 else 3)
            return 0

        lax.fori_loop(0, 2, rest, 0)
        send_parts(2 * group)
        if group == 3:
            work(3 * group + 2, 0, 8, 1)
        send_parts(2 * group + 1)
        if group == 1:
            basis_out[1] = collect(basis_p, basis_out[0], basis_plane)
            for k in range(1, 16):
                basis_a(k).start()
    sums = parts_out[7].astype(F32)
    ups = [e for pair in PAIRS for e in pair if e != 0]
    for e in ups:
        part_copy(e).wait_recv()
        sums = sums + parts_in[7 + e].astype(F32)
    tail = sums[32:48]
    tail = jnp.concatenate([tail, turn(tail)], axis=0)
    top = jnp.concatenate([sums[:32], tail], axis=1)[:, :BLOCK]
    degree = jnp.concatenate([sums[48:49], sums[49:50]], axis=1)[:, :BLOCK]
    diffused = top / degree

    dot_c = lambda a, b: lax.dot_general(
        a, b, (((1,), (1,)), ((), ())), precision=HIGHEST, preferred_element_type=F32
    )
    grams = (wide(dot_c(vec, diffused)), wide(dot_c(diffused, diffused)))
    first = c == 0
    gram_out[3] = jnp.where(first, grams[1], grams[0])
    swap = sib_one(gram_out.at[3], gram_sib.at[0], 1)
    swap.start()
    swap.wait_recv()
    gram_out[0] = jnp.where(first, grams[0], grams[1]) + gram_sib[0]
    for k in range(15, 0, -1):
        gram_p(k).start()
    basis_out[2] = collect(basis_a, basis_out[1], basis_z)
    sib_one(basis_out.at[2], basis_sib, 0).start()
    gram_out[1] = collect(gram_p, gram_out[0], gram_plane)
    for k in sorted(range(1, 16), key=lambda k: -min(k, DEPTH - k)):
        gram_a(k).start()
    sib_one(basis_out.at[2], basis_sib, 0).wait_recv()
    basis = square(basis_out[2] + basis_sib[...])
    gram_out[2] = collect(gram_a, gram_out[1], gram_z)
    swap_back = sib_one(gram_out.at[2], gram_sib.at[1], 2)
    swap_back.start()
    swap_back.wait_recv()
    mine, others = gram_out[2], gram_sib[1]
    coupling = square(jnp.where(first, mine, others))
    diffused_gram = square(jnp.where(first, others, mine))
    dot_t = lambda a, b: lax.dot_general(
        a, b, (((0,), (0,)), ((), ())), precision=HIGHEST, preferred_element_type=F32
    )
    mixed = jnp.dot(basis, coupling, precision=HIGHEST, preferred_element_type=F32)
    spread = diffused_gram + dot_t(
        coupling, mixed * (1.0 / (samples * samples)) - coupling * (2.0 / samples)
    )
    remainder = diffused - dot_t(coupling, vec) * (1.0 / samples)
    factor = lower_inverse(spread)
    out_ref[...] = math.sqrt(samples) * jnp.dot(
        factor, remainder, precision=HIGHEST, preferred_element_type=F32
    )

    for j in range(1, 16):
        src_copy(j).wait_send()
    for j in range(16):
        sib_copy(j).wait_send()
    for e in near + far:
        tgt_copy(e).wait_send()
    for e in ups:
        part_copy(e).wait_send()

    for k in range(1, 16):
        for copy in (basis_p, basis_a, gram_p, gram_a):
            copy(k).wait_send()
    sib_one(basis_out.at[2], basis_sib, 0).wait_send()
    swap.wait_send()
    swap_back.wait_send()


def per_device(descriptors, densities, vectors):
    dma = pltpu.SemaphoreType.DMA
    return pl.pallas_call(
        kernel,
        out_shape=jax.ShapeDtypeStruct((32, BLOCK), F32),
        in_specs=[pl.BlockSpec(memory_space=pl.ANY)] * 3,
        out_specs=pl.BlockSpec(memory_space=pltpu.VMEM),
        scratch_shapes=[
            pltpu.VMEM((32, BLOCK), BF16),
            pltpu.VMEM((1, BLOCK), F32),
            pltpu.VMEM((32, BLOCK), F32),
            pltpu.VMEM((2, 16, 160, 128), BF16),
            pltpu.VMEM((16, 48, 128), BF16),
            pltpu.VMEM((2, 12, 128, 256), BF16),
            pltpu.VMEM((16, 48, 384), BF16),
            pltpu.VMEM((12, 48, 256), F32),
            pltpu.VMEM((16, 64, 128), BF16),
            pltpu.VMEM((16, 64, 128), BF16),
            pltpu.VMEM((3, 8, 128), F32),
            pltpu.VMEM((16, 8, 128), F32),
            pltpu.VMEM((16, 8, 128), F32),
            pltpu.VMEM((8, 128), F32),
            pltpu.VMEM((4, 8, 128), F32),
            pltpu.VMEM((16, 8, 128), F32),
            pltpu.VMEM((16, 8, 128), F32),
            pltpu.VMEM((2, 8, 128), F32),
            dma((3,)),
            *([dma((16,))] * 16),
            dma((3,)), dma((3,)),
        ],
        compiler_params=pltpu.CompilerParams(
            collective_id=0, has_side_effects=True, vmem_limit_bytes=63 << 20
        ),
    )(descriptors, densities.reshape(1, BLOCK), vectors)


def solution(mesh):
    placed = P(None, ("row", "col"))
    return jax.shard_map(
        per_device,
        mesh=mesh,
        in_specs=(placed, P(("row", "col")), placed),
        out_specs=placed,
        check_vma=False,
    )
```

```python
import functools
import math

import jax
import jax.numpy as jnp
from jax import lax
from jax.experimental import pallas as pl
from jax.experimental.pallas import tpu as pltpu
from jax.sharding import PartitionSpec as P

MESH = pl.DeviceIdType.MESH
HIGHEST = lax.Precision.HIGHEST
F32, BF16 = jnp.float32, jnp.bfloat16

BLOCK = 192
PLANE = 16
DEPTH = 16
EXPONENT = math.log2(math.e) / 4.0


def norm_rows(x):
    half = 0.5 * jnp.sum(x * x, axis=0, keepdims=True)
    rest = jnp.broadcast_to(half, (16, half.shape[1]))
    at = lax.broadcasted_iota(jnp.int32, rest.shape, 0)
    rows = jnp.zeros_like(rest)
    for k in range(3):
        piece = rest.astype(BF16).astype(F32)
        rest = rest - piece
        rows = jnp.where(at == k, -piece, rows)
    return rows


def unit_rows(width):
    at = lax.broadcasted_iota(jnp.int32, (16, width), 0)
    return jnp.where(at < 3, 1.0, 0.0)


def lower_inverse(spread):
    n, step = spread.shape[0], 4
    shape = (n, 2 * n)
    at_row = lax.broadcasted_iota(jnp.int32, shape, 0)
    at_col = lax.broadcasted_iota(jnp.int32, shape, 1)
    both = jnp.concatenate([spread, spread], axis=1)
    work = jnp.where(at_col < n, both, jnp.where(at_col - n == at_row, 1.0, 0.0))
    finished = []
    for k in range(0, n, step):
        rows = [work[k + i : k + i + 1] for i in range(step)]
        columns = [jnp.broadcast_to(work[:, k + i : k + i + 1], shape) for i in range(step)]
        for i in range(step):
            pivot = columns[i][k + i : k + i + 1]
            finished.append(rows[i] * lax.rsqrt(pivot))
            share = columns[i] * (1.0 / pivot)
            for j in range(i + 1, step):
                rows[j] = rows[j] - share[k + j : k + j + 1] * rows[i]
                columns[j] = columns[j] - share * columns[i][k + j : k + j + 1]
            work = work - share * rows[i]
    return jnp.concatenate(finished, axis=0)[:, n:]


NEAR = sorted(
    ((dx, dy) for dx in range(4) for dy in range(4)),
    key=lambda o: min(o[0], 4 - o[0]) + min(o[1], 4 - o[1]),
)
PAIRS = ((4, -3), (3, -2), (8, -7), (7, -6), (6, -5), (5, -4), (2, -1), (1, 0))
REACH = 4


def kernel(
    desc_hbm, dens_hbm, vec_hbm, out_ref,
    desc_ref, dens_ref, vec_ref, src, feats, tgt, wts, acc, parts_out, parts_in,
    basis_out, basis_plane, basis_z, basis_sib, gram_out, gram_plane, gram_z, gram_sib,
    in_s, src_s, src_r, sib_s, sib_r, tgt_s, tgt_r, part_s, part_r,
    bp_s, bp_r, bz_s, bz_r, gp_s, gp_r, gz_s, gz_r, one_s, one_r,
):
    loads = [
        pltpu.make_async_copy(there, here, in_s.at[k])
        for k, (there, here) in enumerate(
            ((desc_hbm, desc_ref), (dens_hbm, dens_ref), (vec_hbm, vec_ref))
        )
    ]
    for load in loads:
        load.start()
    row, z = lax.axis_index("row"), lax.axis_index("col")
    p, c = row // 2, row % 2
    px, py = p // 4, p % 4
    other = 1 - c
    samples = float(BLOCK * PLANE * DEPTH * 2)

    def chip(dx, dy):
        return ((px + dx) % 4) * 4 + (py + dy) % 4

    def along(d):
        return (z + d + DEPTH) % DEPTH

    barrier = pltpu.get_barrier_semaphore()

    def greet(device):
        pl.semaphore_signal(barrier, inc=1, device_id=device, device_id_type=MESH)

    for d in range(1, REACH + 1):
        greet((row, along(d)))
        greet((row, along(-d)))
    for dx, dy in NEAR[1:]:
        greet((chip(dx, dy) * 2 + c, z))
    greet((p * 2 + other, z))

    lane16 = lax.broadcasted_iota(jnp.int32, (16, 128), 1)
    at16 = lax.broadcasted_iota(jnp.int32, (16, 128), 0)
    turn = lambda v: pltpu.roll(v, 64, 1)
    pad = lambda v: jnp.concatenate([v, jnp.zeros((v.shape[0], 256 - BLOCK), v.dtype)], axis=1)

    def fold(v):
        return jnp.where(lane16 < 64, v[:16], turn(v[16:]))

    def merge(first, second):
        return jnp.concatenate(
            [jnp.where(lane16 < 64, first, turn(second)), jnp.where(lane16 < 64, turn(first), second)],
            axis=0,
        )

    for load in loads:
        load.wait()
    def wide(v):
        return jnp.concatenate([v[8 * g : 8 * g + 8] for g in range(4)], axis=1)

    def square(v):
        return jnp.concatenate([v[:, 32 * g : 32 * g + 32] for g in range(4)], axis=0)

    x = pad(desc_ref[...].astype(F32))
    feats[7, 0:32] = x[:, :128].astype(BF16)
    feats[7, 32:48] = fold(x[:, 128:]).astype(BF16)
    source = jnp.concatenate([x, norm_rows(x), unit_rows(256)], axis=0)
    later = pltpu.roll(source, 160, 1)
    packed = jnp.concatenate([source[:, :128], later[:, :128]], axis=0).T[:96]
    src[0, 0, 0:96] = packed.astype(BF16)
    vec = vec_ref[...]
    inverse = pad(1.0 / dens_ref[...])
    weighted = pad(vec / dens_ref[...])
    src[0, 0, 96:128] = weighted[:, :128].astype(BF16)
    src[0, 0, 128:144] = fold(weighted[:, 128:]).astype(BF16)
    tail = jnp.broadcast_to(inverse[:, 128:], (16, 128))
    src[0, 0, 144:160] = jnp.where(
        at16 == 0,
        jnp.broadcast_to(inverse[:, :128], (16, 128)),
        jnp.where(at16 == 1, jnp.where(lane16 < 64, tail, turn(tail)), 0.0),
    ).astype(BF16)

    basis_out[0] = wide(
        lax.dot_general(
            vec, vec, (((1,), (1,)), ((), ())), precision=HIGHEST, preferred_element_type=F32
        )
    )
    pl.semaphore_wait(barrier, 2 * REACH + 16)

    def remote(source_ref, target_ref, send_sem, recv_sem, device):
        return pltpu.make_async_remote_copy(
            src_ref=source_ref, dst_ref=target_ref, send_sem=send_sem, recv_sem=recv_sem,
            device_id=device, device_id_type=MESH,
        )

    def src_copy(j):
        return remote(
            src.at[0, 0], src.at[0, j], src_s.at[j], src_r.at[j], (chip(*NEAR[j]) * 2 + c, z)
        )

    def sib_copy(j):
        return remote(
            src.at[0, j], src.at[1, j], sib_s.at[j], sib_r.at[j], (p * 2 + other, z)
        )

    def tgt_copy(e):
        if abs(e) <= REACH:
            return remote(
                feats.at[7], feats.at[7 + e], tgt_s.at[7 + e], tgt_r.at[7 + e], (row, along(-e))
            )
        step = REACH if e > 0 else -REACH
        return remote(
            feats.at[7 + e - step], feats.at[7 + e], tgt_s.at[7 + e], tgt_r.at[7 + e],
            (row, along(-step)),
        )

    def plane_copy(here, there, sends, receives, j):
        return remote(
            here.at[0], there.at[j], sends.at[j], receives.at[j], (chip(*NEAR[j]) * 2 + c, z)
        )

    def z_copy(here, there, sends, receives, k):
        return remote(here.at[1], there.at[k], sends.at[k], receives.at[k], (row, along(k)))

    def sib_one(here, there, k):
        return remote(here, there, one_s.at[k], one_r.at[k], (p * 2 + other, z))

    basis_p = functools.partial(plane_copy, basis_out, basis_plane, bp_s, bp_r)
    basis_a = functools.partial(z_copy, basis_out, basis_z, bz_s, bz_r)
    gram_p = functools.partial(plane_copy, gram_out, gram_plane, gp_s, gp_r)
    gram_a = functools.partial(z_copy, gram_out, gram_z, gz_s, gz_r)

    def collect(copy, own, slots):
        total = own
        for k in range(1, 16):
            copy(k).wait_recv()
            total = total + slots[k]
        return total

    near = [e for d in range(1, REACH + 1) for e in (d, -d)]
    far = [e for d in range(1, REACH + 1) for e in (d + REACH, -d - REACH) if e > -8]
    for j in range(1, 5):
        src_copy(j).start()
    for e in reversed(near):
        tgt_copy(e).start()
    sib_copy(0).start()
    for j in range(5, 16):
        src_copy(j).start()
    acc[...] = jnp.zeros_like(acc)
    def arrive(m):
        for j in range(4 * m, 4 * m + 4):
            if j > 0:
                src_copy(j).wait_recv()
                sib_copy(j).start()

    arrive(0)
    for e in near:
        tgt_copy(e).wait_recv()
        ahead = e + (REACH if e > 0 else -REACH)
        if ahead in far:
            tgt_copy(ahead).start()

    unit_tile = unit_rows(128)
    zeros = jnp.zeros((64, 128), F32)

    def build(pair):
        first, second = (feats[7 + e].astype(F32) for e in PAIRS[pair])
        for t, tile in enumerate((first[:32], second[:32], merge(first[32:], second[32:]))):
            rows = jnp.concatenate([tile, unit_tile, norm_rows(tile)], axis=0)
            k = 3 * pair + t
            at = slice(128 * (k % 2), 128 * (k % 2) + 128)
            tgt[0, k // 2, :, at] = jnp.concatenate([rows, zeros], axis=0).astype(BF16)
            tgt[1, k // 2, :, at] = jnp.concatenate([zeros, rows], axis=0).astype(BF16)

    for pair in range(2):
        build(pair)

    def columns(j):
        first, second = src[0, j], src[1, j]
        wts[j, :, 0:128] = jnp.concatenate([first[96:128], first[144:160]], axis=0)
        wts[j, :, 128:256] = jnp.concatenate([second[96:128], second[144:160]], axis=0)
        tails = merge(first[128:144].astype(F32), second[128:144].astype(F32))
        ends = jnp.where(
            lane16 < 64, first[144:160].astype(F32), second[144:160].astype(F32)
        )
        ends = jnp.where(at16 == 0, jnp.broadcast_to(ends[1:2], (16, 128)), 0.0)
        wts[j, :, 256:384] = jnp.concatenate([tails, ends], axis=0).astype(BF16)

    def work(first_chunk, first_chip, pairs, chunks=3):
        units = [(k, n) for k in range(chunks) for n in range(pairs)]
        inner, kernels = {}, {}
        for i in range(len(units) + 2):
            if i < len(units):
                k, n = units[i]
                rows = jnp.concatenate(
                    [src[s, first_chip + 2 * n + j, 0:96] for j in range(2) for s in range(2)], axis=0
                )
                inner[i] = [
                    jnp.dot(rows, tgt[v, first_chunk + k], preferred_element_type=F32)
                    for v in range(2)
                ]
            if 0 <= i - 1 < len(units):
                low, high = (
                    jnp.exp2(u * F32(EXPONENT)).astype(BF16) for u in inner.pop(i - 1)
                )
                order = []
                for j in range(2):
                    a, b = 192 * j, 192 * j + 96
                    order += [
                        low[a : a + 96], high[a : a + 32], low[b : b + 96], high[b : b + 32],
                        high[a + 32 : a + 96], high[b + 32 : b + 96],
                    ]
                kernels[i - 1] = jnp.concatenate(order, axis=0)
            if 0 <= i - 2 < len(units):
                k, n = units[i - 2]
                weights = jnp.concatenate(
                    [wts[first_chip + 2 * n + j] for j in range(2)], axis=1
                )
                acc[first_chunk + k] += jnp.dot(
                    weights, kernels.pop(i - 2), preferred_element_type=F32
                )

    def part_copy(e):
        return remote(
            parts_out.at[7 + e], parts_in.at[7 + e], part_s.at[7 + e], part_r.at[7 + e],
            (row, along(e)),
        )

    def send_parts(pair):
        tiles = [
            acc[k // 2, :, 128 * (k % 2) : 128 * (k % 2) + 128]
            for k in range(3 * pair, 3 * pair + 3)
        ]
        both = tiles[2]
        for s, e in enumerate(PAIRS[pair]):
            tail = turn(both) if s else both
            parts_out[7 + e, 0:32] = tiles[s][:32].astype(BF16)
            parts_out[7 + e, 32:48] = fold(tail[:32]).astype(BF16)
            parts_out[7 + e, 48:64] = jnp.where(
                at16 == 0,
                jnp.broadcast_to(tiles[s][32:33], (16, 128)),
                jnp.broadcast_to(tail[32:33], (16, 128)),
            ).astype(BF16)
            if e != 0:
                part_copy(e).start()

    for m in range(4):
        if m < 3:
            arrive(m + 1)
        for j in range(4 * m, 4 * m + 4):
            sib_copy(j).wait_recv()
            columns(j)
        if m == 3:
            for j in range(1, 16):
                basis_p(j).start()
        work(0, 4 * m, 2)
    for pair in range(2):
        send_parts(pair)
    for e in far:
        tgt_copy(e).wait_recv()
    for group in range(1, 4):
        for pair in (2 * group, 2 * group + 1):
            build(pair)

        def rest(m, _):
            work(3 * group, 8 * m, 4, 2 if group == 3 else 3)
            return 0

        lax.fori_loop(0, 2, rest, 0)
        send_parts(2 * group)
        if group == 3:
            work(3 * group + 2, 0, 8, 1)
        send_parts(2 * group + 1)
        if group == 1:
            basis_out[1] = collect(basis_p, basis_out[0], basis_plane)
            for k in range(1, 16):
                basis_a(k).start()
    sums = parts_out[7].astype(F32)
    ups = [e for pair in PAIRS for e in pair if e != 0]
    for e in ups:
        part_copy(e).wait_recv()
        sums = sums + parts_in[7 + e].astype(F32)
    tail = sums[32:48]
    tail = jnp.concatenate([tail, turn(tail)], axis=0)
    top = jnp.concatenate([sums[:32], tail], axis=1)[:, :BLOCK]
    degree = jnp.concatenate([sums[48:49], sums[49:50]], axis=1)[:, :BLOCK]
    diffused = top / degree

    dot_c = lambda a, b: lax.dot_general(
        a, b, (((1,), (1,)), ((), ())), precision=HIGHEST, preferred_element_type=F32
    )
    grams = (wide(dot_c(vec, diffused)), wide(dot_c(diffused, diffused)))
    first = c == 0
    gram_out[3] = jnp.where(first, grams[1], grams[0])
    swap = sib_one(gram_out.at[3], gram_sib.at[0], 1)
    swap.start()
    swap.wait_recv()
    gram_out[0] = jnp.where(first, grams[0], grams[1]) + gram_sib[0]
    for k in range(15, 0, -1):
        gram_p(k).start()
    basis_out[2] = collect(basis_a, basis_out[1], basis_z)
    sib_one(basis_out.at[2], basis_sib, 0).start()
    gram_out[1] = collect(gram_p, gram_out[0], gram_plane)
    for k in sorted(range(1, 16), key=lambda k: -min(k, DEPTH - k)):
        gram_a(k).start()
    sib_one(basis_out.at[2], basis_sib, 0).wait_recv()
    basis = square(basis_out[2] + basis_sib[...])
    gram_out[2] = collect(gram_a, gram_out[1], gram_z)
    swap_back = sib_one(gram_out.at[2], gram_sib.at[1], 2)
    swap_back.start()
    swap_back.wait_recv()
    mine, others = gram_out[2], gram_sib[1]
    coupling = square(jnp.where(first, mine, others))
    diffused_gram = square(jnp.where(first, others, mine))
    dot_t = lambda a, b: lax.dot_general(
        a, b, (((0,), (0,)), ((), ())), precision=HIGHEST, preferred_element_type=F32
    )
    mixed = jnp.dot(basis, coupling, precision=HIGHEST, preferred_element_type=F32)
    spread = diffused_gram + dot_t(
        coupling, mixed * (1.0 / (samples * samples)) - coupling * (2.0 / samples)
    )
    remainder = diffused - dot_t(coupling, vec) * (1.0 / samples)
    factor = lower_inverse(spread)
    out_ref[...] = math.sqrt(samples) * jnp.dot(
        factor, remainder, precision=HIGHEST, preferred_element_type=F32
    )

    for j in range(1, 16):
        src_copy(j).wait_send()
    for j in range(16):
        sib_copy(j).wait_send()
    for e in near + far:
        tgt_copy(e).wait_send()
    for e in ups:
        part_copy(e).wait_send()

    for k in range(1, 16):
        for copy in (basis_p, basis_a, gram_p, gram_a):
            copy(k).wait_send()
    sib_one(basis_out.at[2], basis_sib, 0).wait_send()
    swap.wait_send()
    swap_back.wait_send()


def per_device(descriptors, densities, vectors):
    dma = pltpu.SemaphoreType.DMA
    return pl.pallas_call(
        kernel,
        out_shape=jax.ShapeDtypeStruct((32, BLOCK), F32),
        in_specs=[pl.BlockSpec(memory_space=pl.ANY)] * 3,
        out_specs=pl.BlockSpec(memory_space=pltpu.VMEM),
        scratch_shapes=[
            pltpu.VMEM((32, BLOCK), BF16),
            pltpu.VMEM((1, BLOCK), F32),
            pltpu.VMEM((32, BLOCK), F32),
            pltpu.VMEM((2, 16, 160, 128), BF16),
            pltpu.VMEM((16, 48, 128), BF16),
            pltpu.VMEM((2, 12, 128, 256), BF16),
            pltpu.VMEM((16, 48, 384), BF16),
            pltpu.VMEM((12, 48, 256), F32),
            pltpu.VMEM((16, 64, 128), BF16),
            pltpu.VMEM((16, 64, 128), BF16),
            pltpu.VMEM((3, 8, 128), F32),
            pltpu.VMEM((16, 8, 128), F32),
            pltpu.VMEM((16, 8, 128), F32),
            pltpu.VMEM((8, 128), F32),
            pltpu.VMEM((4, 8, 128), F32),
            pltpu.VMEM((16, 8, 128), F32),
            pltpu.VMEM((16, 8, 128), F32),
            pltpu.VMEM((2, 8, 128), F32),
            dma((3,)),
            *([dma((16,))] * 16),
            dma((3,)), dma((3,)),
        ],
        compiler_params=pltpu.CompilerParams(
            collective_id=0, has_side_effects=True, vmem_limit_bytes=63 << 20
        ),
    )(descriptors, densities.reshape(1, BLOCK), vectors)


def solution(mesh):
    placed = P(None, ("row", "col"))
    return jax.shard_map(
        per_device,
        mesh=mesh,
        in_specs=(placed, P(("row", "col")), placed),
        out_specs=placed,
        check_vma=False,
    )
```
